32 devices in a mesh: dp: 4 (over z), seq: 2 (over y), tile: 4 (over x, core).
Axes of the slice: x: 2, y: 2, z: 4, core: 2. Of those that a mesh axis runs over, the one named last changes fastest.
Arguments:
- latents: bfloat16 [4, 2, 512, 1152], P('dp', 'seq', 'tile'), may hold values from -6 to 6
- upstream: bfloat16 [4, 2, 512, 1152], P('dp', 'seq', 'tile'), may hold values from -6 to 6
- modulation: float32 [4, 2, 1152], P('dp'), may hold values from -0.5 to 6
- space_qkv: bfloat16 [1152, 1728], P(('dp', 'tile')), may hold values from -1 to 1
- space_out: bfloat16 [576, 1152], P(('dp', 'tile')), may hold values from -0.25 to 0.25
- time_qkv: bfloat16 [1152, 1728], P(('dp', 'tile')), may hold values from -1 to 1
- time_out: bfloat16 [576, 1152], P(('dp', 'tile')), may hold values from -0.25 to 0.25
- space_pattern: int32 [8, 4], P('tile'), may hold values 0 or 1
- time_mask: int32 [2, 2], replicated, may hold values 0 or 1
Outputs:
- result: bfloat16 [4, 2, 512, 1152], P('dp', 'seq', 'tile')
- start_grad: bfloat16 [4, 2, 512, 1152], P('dp', 'seq', 'tile')
- time_out_grad: float32 [576, 1152], P(('dp', 'tile'))
The draws below stay inside these ranges and needn't reach their ends.
All inputs are finite; a program needn't handle non-finite values. No bound on the sum of `space_pattern` on one device may be relied on, other than what follows from the above.
Results may differ from the reference program's by a relative error of at most 0.035.
Values may be sent and summed in bfloat16 or wider, within the bound.
No kernel may reach another device: no remote copies, remote signals or barrier semaphores. Data moves between devices by JAX's collectives and lax.ppermute only.
A program may use at most 64 MiB of HBM per device.

```python
import jax
import jax.numpy as jnp
from jax import lax

D = 1152
HEADS = 8
HEAD_DIM = 72
SBLK = 64
CLIPS = 4
FRAMES = 2
PATCHES = 512


def qkv_columns(key):
    parts = jax.random.normal(key, (3, D, HEADS * HEAD_DIM), jnp.float32)
    parts = jnp.clip(parts, -6.0, 6.0)
    mixed = parts[1]
    whole = jnp.concatenate([parts[0], mixed, parts[2]], axis=1)
    return whole * D ** (-0.5)


def draw_modulation(key, part):
    key = jax.random.fold_in(key, 11)
    values = jax.random.uniform(key, (CLIPS, 2, D), jnp.float32, -0.5, 1.0)
    return values


def draw_space_qkv(key, part):
    key = jax.random.fold_in(key, 21)
    whole = qkv_columns(key)
    return whole.astype(jnp.bfloat16)


def draw_time_qkv(key, part):
    key = jax.random.fold_in(key, 31)
    whole = qkv_columns(key)
    return whole.astype(jnp.bfloat16)


def with_ends(values, own_key, smallest, largest):
    shape = values.shape
    spot = [jax.random.randint(jax.random.fold_in(own_key, axis), (), 0, shape[axis]) for axis in range(len(shape))]
    values = values.at[tuple(spot)].set(smallest)
    longest = shape.index(max(shape))
    spot[longest] = (spot[longest] + 1) % shape[longest]
    return values.at[tuple(spot)].set(largest)


def levels(own_key, shape, shards, smallest, largest):
    level, own = 1.0, jax.random.fold_in(own_key, 6)
    for axis_at, blocks in shards:
        steps = jnp.exp(jax.random.uniform(jax.random.fold_in(own, axis_at), (blocks,), jnp.float32, smallest / len(shards), largest / len(shards)))
        level = level * jnp.repeat(steps, shape[axis_at] // blocks).reshape([-1 if axis == axis_at else 1 for axis in range(len(shape))])
    return level


def scatter_about(own_key, dims, scale, most, cuts=(), kind=jnp.bfloat16):
    level = levels(own_key, dims, cuts, -0.22, 0.18) if cuts else 1.0
    entries = jax.random.normal(own_key, dims, jnp.float32) * scale * level
    return jnp.minimum(jnp.maximum(entries, -most), most).astype(kind)


def setup_inputs(seed: int = 0) -> dict:
    arg_keys = jax.random.split(jax.random.key(seed), 10)
    latents = scatter_about(arg_keys[0], (CLIPS, FRAMES, PATCHES, D), 1.0, 6.0, ((0, 4), (1, 2), (2, 4)))
    upstream = scatter_about(arg_keys[1], (CLIPS, FRAMES, PATCHES, D), 1.0, 6.0, ((0, 4), (1, 2), (2, 4)))
    modulation = draw_modulation(jax.random.fold_in(arg_keys[9], 71), 0)
    space_qkv = draw_space_qkv(jax.random.fold_in(arg_keys[9], 71), 0)
    space_out = scatter_about(arg_keys[4], (HEADS * HEAD_DIM, D), (HEADS * HEAD_DIM) ** -0.5, 0.25, ((0, 16),))
    time_qkv = draw_time_qkv(jax.random.fold_in(arg_keys[9], 71), 0)
    time_out = scatter_about(arg_keys[6], (HEADS * HEAD_DIM, D), (HEADS * HEAD_DIM) ** -0.5, 0.25, ((0, 16),))
    space_pattern = with_ends((jax.random.randint(arg_keys[7], (PATCHES // SBLK, 4), 0, 4) < 3).astype(jnp.int32), jax.random.fold_in(arg_keys[7], 1), 0, 1)
    time_mask = with_ends((jax.random.randint(arg_keys[8], (FRAMES, FRAMES), 0, 4) < 3).astype(jnp.int32), jax.random.fold_in(arg_keys[8], 1), 0, 1)
    return dict(latents=latents, upstream=upstream, modulation=modulation, space_qkv=space_qkv, space_out=space_out, time_qkv=time_qkv, time_out=time_out, space_pattern=space_pattern, time_mask=time_mask)


EPSILON = 1e-06
MASKED = -1e+30

def heads(rows):
    return rows.reshape(rows.shape[:-1] + (HEADS, HEAD_DIM))

def merged(rows):
    return rows.reshape(rows.shape[:-2] + (HEADS * HEAD_DIM,))

def split(rows):
    width = HEADS * HEAD_DIM
    return (heads(rows[..., :width]), heads(rows[..., width:2 * width]), heads(rows[..., 2 * width:]))

def project(rows, weight):
    flat = rows.reshape(-1, rows.shape[-1])
    out = jnp.dot(flat, weight, preferred_element_type=jnp.float32)
    return out.reshape(rows.shape[:-1] + (weight.shape[1],))

def norm_scale(values, gain):
    inverse = lax.rsqrt(lax.optimization_barrier(jnp.mean(values * values, axis=-1, keepdims=True)) + EPSILON)
    return (inverse, values * inverse * gain)

def norm_back(values, inverse, gain, grad):
    scaled = grad * gain
    cubed = inverse * inverse * inverse
    return inverse * scaled - values * cubed * lax.optimization_barrier(jnp.mean(scaled * values, axis=-1, keepdims=True))

def forms(lead):
    if lead:
        return ('cbqhe', 'cbkhe')
    return ('cqbhe', 'ckbhe')

def weights_of(query, keys, allowed, lead):
    qform, kform = forms(lead)
    scores = jnp.einsum(qform + ',' + kform + '->cbhqk', query.astype(jnp.float32), keys.astype(jnp.float32))
    scores = jnp.where(allowed, scores * HEAD_DIM ** (-0.5), MASKED)
    top = lax.optimization_barrier(jnp.max(scores, axis=-1, keepdims=True))
    raised = jnp.exp(scores - top)
    return raised / lax.optimization_barrier(jnp.sum(raised, axis=-1, keepdims=True))

def attend(query, keys, values, allowed, lead):
    qform, kform = forms(lead)
    probs = weights_of(query, keys, allowed, lead)
    rounded = probs.astype(jnp.bfloat16).astype(jnp.float32)
    out = jnp.einsum('cbhqk,' + kform + '->' + qform, rounded, values.astype(jnp.float32))
    return (out.astype(jnp.bfloat16), probs)

def attend_back(query, keys, values, probs, grad_out, lead):
    qform, kform = forms(lead)
    grad32 = grad_out.astype(jnp.float32)
    dprob = jnp.einsum(qform + ',' + kform + '->cbhqk', grad32, values.astype(jnp.float32))
    delta = lax.optimization_barrier(jnp.sum(probs * dprob, axis=-1, keepdims=True))
    dscore = (probs * (dprob - delta) * HEAD_DIM ** (-0.5)).astype(jnp.bfloat16).astype(jnp.float32)
    dquery = jnp.einsum('cbhqk,' + kform + '->' + qform, dscore, keys.astype(jnp.float32))
    dkeys = jnp.einsum('cbhqk,' + qform + '->' + kform, dscore, query.astype(jnp.float32))
    rounded = probs.astype(jnp.bfloat16).astype(jnp.float32)
    dvalues = jnp.einsum('cbhqk,' + qform + '->' + kform, rounded, grad32)
    return (dquery, dkeys, dvalues)

def space_ok(space_pattern):
    block = jnp.arange(PATCHES) // SBLK
    rel = block[None, :] - 2 * (block[:, None] // 2) + 1
    inside = (rel >= 0) & (rel < 4)
    picked = jnp.take_along_axis(space_pattern[block], jnp.clip(rel, 0, 3), axis=1)
    return inside & ((picked == 1) | (block[None, :] == block[:, None]))

def time_ok(time_mask):
    frame = jnp.arange(FRAMES)
    return (frame[None, :] == frame[:, None]) | (frame[None, :] < frame[:, None]) & (time_mask == 1)

def reference(latents, upstream, modulation, space_qkv, space_out, time_qkv, time_out, space_pattern, time_mask):
    width = HEADS * HEAD_DIM
    start = latents.astype(jnp.float32)
    gain_space = 1.0 + modulation[:, 0][:, None, None, :]
    gain_time = 1.0 + modulation[:, 1][:, None, None, :]
    inverse_space, normed = norm_scale(start, gain_space)
    space_rows = project(normed.astype(jnp.bfloat16), space_qkv).astype(jnp.bfloat16)
    space_mask = space_ok(space_pattern)[None, None, None]
    frames_flat = space_rows.reshape(CLIPS * FRAMES, PATCHES, 3 * width)

    def space_forward(block):
        query, keys, values = split(block[None, None])
        out, probs = attend(query, keys, values, space_mask, True)
        return merged(out)[0, 0]
    space_att = lax.map(space_forward, frames_flat).reshape(CLIPS, FRAMES, PATCHES, width)
    middle = start + project(space_att, space_out)
    inverse_time, normed_time = norm_scale(middle, gain_time)
    time_rows = project(normed_time.astype(jnp.bfloat16), time_qkv).astype(jnp.bfloat16)
    frame_mask = time_ok(time_mask)[None, None, None]
    time_query, time_keys, time_values = split(time_rows)
    time_heads, time_probs = attend(time_query, time_keys, time_values, frame_mask, False)
    time_att = merged(time_heads)
    result = (middle + project(time_att, time_out)).astype(jnp.bfloat16)
    flat_up = upstream.reshape(-1, D)
    time_out_grad = jnp.dot(time_att.reshape(-1, width).T, flat_up, preferred_element_type=jnp.float32)
    grad_att = project(upstream, time_out.T).astype(jnp.bfloat16)
    gq, gk, gv = attend_back(time_query, time_keys, time_values, time_probs, heads(grad_att), False)
    time_grads = jnp.concatenate([merged(gq), merged(gk), merged(gv)], axis=-1).astype(jnp.bfloat16)
    middle_grad = upstream.astype(jnp.float32) + norm_back(middle, inverse_time, gain_time, project(time_grads, time_qkv.T))
    space_grad_att = project(middle_grad.astype(jnp.bfloat16), space_out.T).astype(jnp.bfloat16)
    grads_flat = space_grad_att.reshape(CLIPS * FRAMES, PATCHES, width)

    def space_backward(pair):
        block, grad = pair
        query, keys, values = split(block[None, None])
        probs = weights_of(query, keys, space_mask, True)
        dq, dk, dv = attend_back(query, keys, values, probs, heads(grad[None, None]), True)
        return jnp.concatenate([merged(dq), merged(dk), merged(dv)], axis=-1)[0, 0].astype(jnp.bfloat16)
    space_grads = lax.map(space_backward, (frames_flat, grads_flat)).reshape(CLIPS, FRAMES, PATCHES, 3 * width)
    start_grad = middle_grad + norm_back(start, inverse_space, gain_space, project(space_grads, space_qkv.T))
    return (result, start_grad.astype(jnp.bfloat16), time_out_grad)
```

```python
import functools

import jax
import jax.numpy as jnp
import numpy as np
from jax import lax
from jax.experimental import pallas as pl
from jax.experimental.pallas import tpu as pltpu
from jax.sharding import PartitionSpec as P

HEADS = 8
HEAD_DIM = 72
WIDTH = HEADS * HEAD_DIM
EPSILON = 1e-06
MASKED = -1e30
SCALE = HEAD_DIM ** (-0.5)
BF16 = jnp.bfloat16
F32 = jnp.float32
VMEM_LIMIT = 16 * 1024 * 1024
PACK_LIMIT = 63 * 1024 * 1024


def mm(a, b):
    return jnp.dot(a, b, preferred_element_type=F32)


def mm_nt(a, b):
    return lax.dot_general(a, b, (((1,), (1,)), ((), ())), preferred_element_type=F32)


def mm_tn(a, b):
    return lax.dot_general(a, b, (((0,), (0,)), ((), ())), preferred_element_type=F32)


def head_masks(kind):
    lane = lax.broadcasted_iota(jnp.int32, (1, WIDTH), 1)
    inside = [(lane >= HEAD_DIM * h) & (lane < HEAD_DIM * (h + 1)) for h in range(HEADS)]
    return [jnp.where(hit, 1.0, 0.0).astype(kind) for hit in inside]


def spread(rows):
    return jnp.concatenate([rows * mask for mask in head_masks(rows.dtype)], axis=0)


def collect(big):
    n = big.shape[0] // HEADS
    masks = head_masks(F32)
    total = big[:n] * masks[0]
    for h in range(1, HEADS):
        total = total + big[h * n : (h + 1) * n] * masks[h]
    return total


def softmax_of(spread_q, keys, allowed):
    n, m = allowed.shape
    scores = (mm_nt(spread_q, keys) * SCALE).reshape(HEADS, n, m)
    scores = jnp.where((allowed > 0)[None], scores, MASKED)
    raised = jnp.exp(scores - jnp.max(scores, axis=-1, keepdims=True))
    probs = raised / jnp.sum(raised, axis=-1, keepdims=True)
    return probs.reshape(HEADS * n, m)


def attention_back(spread_q, keys, values, probs, grad):
    spread_g = spread(grad)
    dprob = mm_nt(spread_g, values)
    delta = jnp.sum(probs * dprob, axis=-1, keepdims=True)
    dscore = (probs * (dprob - delta) * SCALE).astype(BF16)
    dquery = collect(mm(dscore, keys))
    dkeys = mm_tn(dscore, spread_q)
    dvalues = mm_tn(probs.astype(BF16), spread_g)
    return dquery, dkeys, dvalues


def inverse_of(values):
    return lax.rsqrt(jnp.mean(values * values, axis=-1, keepdims=True) + EPSILON)


def norm_back(values, gain, grad):
    inverse = inverse_of(values)
    scaled = grad * gain
    cubed = inverse * inverse * inverse
    return inverse * scaled - values * cubed * jnp.mean(scaled * values, axis=-1, keepdims=True)


def expander(source, rows=WIDTH):
    row = lax.broadcasted_iota(jnp.int32, (rows, source.shape[1]), 0)
    return jnp.where(row == source, 1.0, 0.0).astype(BF16)


def ahead(rows, weight, start, stop, slots):
    total = None
    for (at, count), ref in zip(slots, weight):
        term = mm(rows[:, at : at + count], ref[:, start:stop])
        total = term if total is None else total + term
    return total


def behind(grad, weight, start, stop, select, rounded=False):
    count = grad.shape[0]
    turned = grad.astype(F32).T.astype(BF16)
    parts = [mm(ref[:, start:stop], turned) for ref in weight]
    part = jnp.concatenate(parts, axis=0)
    high = part.astype(BF16)
    if rounded:
        return mm(select[...], high).T.astype(BF16)
    low = (part - high.astype(F32)).astype(BF16)
    both = mm(select[...], jnp.concatenate([high, low], axis=1))
    return (both[:, :count] + both[:, count:]).T


def space_allowed(place, pattern, span, tiles):
    own = 2 * span
    row = lax.broadcasted_iota(jnp.int32, (own, 4 * span), 0)
    column = lax.broadcasted_iota(jnp.int32, (own, 4 * span), 1)
    tile_at = place[0]
    allowed = jnp.zeros((own, 4 * span), jnp.int32)
    for b in range(2):
        for r in range(4):
            block = 2 * tile_at - 1 + r
            inside = (block >= 0) & (block < 2 * tiles)
            seen = inside if r == b + 1 else inside & (pattern[b, r] == 1)
            here = (row >= b * span) & (row < (b + 1) * span)
            here = here & (column >= r * span) & (column < (r + 1) * span)
            allowed = allowed + jnp.where(here, seen.astype(jnp.int32), 0)
    return allowed


def fetch(sources, buffers, semaphores):
    copies = [
        pltpu.make_async_copy(source, buffer, semaphores.at[number])
        for number, (source, buffer) in enumerate(zip(sources, buffers))
    ]
    for copy in copies:
        copy.start()
    for copy in copies:
        copy.wait()


def columns(model):
    wide = -(-3 * WIDTH // 128) * 128
    return 0, wide, 2 * wide, 2 * wide + model


def pack_kernel(
    space_hbm, time_hbm, space_out_hbm, time_out_hbm, packed, half_ref,
    space_qkv, time_qkv, space_out, time_out, ready,
):
    fetch(
        (space_hbm, time_hbm, space_out_hbm, time_out_hbm),
        (space_qkv, time_qkv, space_out, time_out), ready,
    )
    outs = jnp.concatenate([space_out[...].astype(F32), time_out[...].astype(F32)], axis=0)
    parts = [space_qkv[...].astype(F32), time_qkv[...].astype(F32), outs]
    packed[...] = jnp.concatenate(parts, axis=1).astype(BF16)
    lanes = half_ref.shape[1]
    first = lax.axis_index("seq") == 0

    @pl.when(first)
    def _():
        half_ref[...] = packed[:, :lanes]

    @pl.when(jnp.logical_not(first))
    def _():
        half_ref[...] = packed[:, lanes:]


def send_kernel(cut, piece, by_tile, by_seq, over_tile, over_seq):
    at, lanes = 0, cut[1]
    if piece is not None:
        at = piece.shape[1]
        over_tile[:, :at] = piece[...]
        over_seq[:, :at] = piece[...]
    over_tile[:, at:] = by_seq[:, : cut[0]]
    over_seq[:, at:] = by_tile[:, cut[0] : lanes]


def place_columns(out_ref, row, full):
    rows = slice(row, row + full.shape[0])
    space, time, out, stop = columns(full.shape[1] - 6 * WIDTH)
    pad = jnp.zeros((full.shape[0], time - space - 3 * WIDTH), BF16)
    out_ref[rows, space : space + 3 * WIDTH] = full[:, : 3 * WIDTH].astype(BF16)
    out_ref[rows, space + 3 * WIDTH : time] = pad
    out_ref[rows, time : time + 3 * WIDTH] = full[:, 3 * WIDTH : 6 * WIDTH].astype(BF16)
    out_ref[rows, time + 3 * WIDTH : out] = pad
    out_ref[rows, out:stop] = full[:, 6 * WIDTH :].astype(BF16)


def join_kernel(owned, place, *refs):
    whole, parts, out_ref = refs[:owned], refs[owned:-1], refs[-1]
    top = 0
    if whole:
        rows = [ref[...].astype(F32) for ref in whole]
        place_columns(out_ref, 0, jnp.concatenate(rows, axis=0))
        top = sum(ref.shape[0] for ref in whole)
    if not parts:
        return
    near, by_tile, by_seq, corner_low, corner_high = parts
    lanes = near.shape[1]
    mine = [near[...].astype(F32), by_tile[:, :lanes].astype(F32)]
    mine = jnp.concatenate(mine, axis=0)
    low, high = corner_low.shape[1] % lanes, corner_high.shape[1] % lanes
    corner = [
        corner_low[:, corner_low.shape[1] - low :].astype(F32),
        corner_high[:, corner_high.shape[1] - high :].astype(F32),
    ]
    corner = jnp.concatenate(corner, axis=1)
    other = jnp.concatenate([by_seq[:, :lanes].astype(F32), corner], axis=0)

    @pl.when(place[1] == 0)
    def _():
        place_columns(out_ref, top, jnp.concatenate([mine, other], axis=1))

    @pl.when(place[1] != 0)
    def _():
        place_columns(out_ref, top, jnp.concatenate([other, mine], axis=1))


def order_kernel(index_ref, order_ref):
    order_ref[...] = expander(index_ref[0:1, :], order_ref.shape[0])


def normed_kernel(order_ref, before, x_ref, after, mod_ref, normed_ref):
    x = jnp.concatenate([before[...], x_ref[...], after[...]], axis=0).astype(F32)
    normed = (x * inverse_of(x) * (1.0 + mod_ref[0:1, :])).astype(BF16)
    normed_ref[...] = mm(normed, order_ref[...]).astype(BF16)


def early_kernel(slots, normed_ref, weight, partial_ref):
    partial_ref[...] = ahead(normed_ref, weight, 0, 3 * WIDTH, slots)


def forward_kernel(tiles, slots, late, place, pattern, normed_ref, *refs):
    *partial, weight, q_ref, kv_ref, att_ref = refs
    own = q_ref.shape[0]
    span = own // 2
    rows = ahead(
        normed_ref, [weight[n] for n in late], 0, 3 * WIDTH, [slots[n] for n in late]
    )
    for earlier in partial:
        rows = rows + earlier[...]
    rows = rows.astype(BF16)
    query, kv = rows[span : span + own, :WIDTH], rows[:, WIDTH:]
    keys, values = kv[:, :WIDTH], kv[:, WIDTH:]
    q_ref[...] = query
    kv_ref[...] = kv
    allowed = space_allowed(place, pattern, span, tiles)
    probs = softmax_of(spread(query), keys, allowed)
    att_ref[...] = collect(mm(probs.astype(BF16), values)).astype(BF16)


def middle_of(slots, index_ref, order_ref, x_ref, mod_ref, att, weight):
    _, time, out, stop = columns(x_ref.shape[1])
    att = mm(att, expander(index_ref[1:2, :])).astype(BF16)
    middle = x_ref[...].astype(F32) + ahead(att, weight, out, stop, slots)
    normed = (middle * inverse_of(middle) * (1.0 + mod_ref[1:2, :])).astype(BF16)
    normed = mm(normed, order_ref[...]).astype(BF16)
    return middle, ahead(normed, weight, time, time + 3 * WIDTH, slots).astype(BF16)


def middle_kernel(slots, index_ref, order_ref, x_ref, mod_ref, att_ref, weight, middle_ref, rows_ref):
    middle, rows = middle_of(slots, index_ref, order_ref, x_ref, mod_ref, att_ref[...], weight)
    middle_ref[...] = middle
    rows_ref[...] = rows


def att_grad_kernel(parts, row, index_ref, *refs):
    upstream = jnp.concatenate([ref[...] for ref in refs[:parts]], axis=0).astype(BF16)
    weight, grad_ref = refs[parts:]
    *_, out, stop = columns(upstream.shape[1])
    grad_ref[...] = behind(
        upstream, weight, out, stop, expander(index_ref[row : row + 1, :]), rounded=True
    )


def time_att_kernel(allowed_ref, rows_ref, grad_ref, out_ref):
    rows = rows_ref[...]
    query, keys, values = rows[:, :WIDTH], rows[:, WIDTH : 2 * WIDTH], rows[:, 2 * WIDTH :]
    spread_q = spread(query)
    probs = softmax_of(spread_q, keys, allowed_ref[...])
    att = collect(mm(probs.astype(BF16), values))
    grads = attention_back(spread_q, keys, values, probs, grad_ref[...])
    out_ref[...] = jnp.concatenate(grads + (att,), axis=1).astype(BF16)


def time_pair_kernel(
    slots, place, time_mask, index_ref, order_ref, mod_ref, x_ref, space_ref, own_ref, grad_ref,
    weight, out_ref, att_ref,
):
    count = own_ref.shape[0]
    first = place[1] == 0

    def frames(own, other):
        own, other = own.astype(F32), other.astype(F32)
        return jnp.where(first, own, other), jnp.where(first, other, own)

    _, other = middle_of(slots, index_ref, order_ref, x_ref, mod_ref, space_ref[...], weight)
    own = own_ref[...]
    row = lax.broadcasted_iota(jnp.int32, (WIDTH, 128), 0)
    low = lax.broadcasted_iota(jnp.int32, (WIDTH, 128), 1) * HEAD_DIM
    heads = jnp.where((row >= low) & (row < low + HEAD_DIM), 1.0, 0.0).astype(BF16)

    def summed(product):
        high = product.astype(BF16)
        return mm(high, heads) + mm((product - high.astype(F32)).astype(BF16), heads)

    def widened(value):
        return mm_nt(value.astype(BF16), heads)

    _, q1 = frames(own[:, :WIDTH], other[:, :WIDTH])
    k0, k1 = frames(own[:, WIDTH : 2 * WIDTH], other[:, WIDTH : 2 * WIDTH])
    v0, v1 = frames(own[:, 2 * WIDTH :], other[:, 2 * WIDTH :])
    g0, g1 = frames(grad_ref[:count, :], grad_ref[count:, :])
    s10 = jnp.where(time_mask[1, 0] == 1, summed(q1 * k0) * SCALE, MASKED)
    s11 = summed(q1 * k1) * SCALE
    top = jnp.maximum(s10, s11)
    e10, e11 = jnp.exp(s10 - top), jnp.exp(s11 - top)
    total = e10 + e11
    p10, p11 = e10 / total, e11 / total
    dp10, dp11 = summed(g1 * v0), summed(g1 * v1)
    delta = p10 * dp10 + p11 * dp11
    d10, d11 = widened(p10 * (dp10 - delta) * SCALE), widened(p11 * (dp11 - delta) * SCALE)
    w10, w11 = widened(p10), widened(p11)
    att1 = w10 * v0 + w11 * v1
    zero = jnp.zeros_like(q1)
    of_frame0 = (zero, d10 * q1, g0 + w10 * g1, v0)
    of_frame1 = (d10 * k0 + d11 * k1, d11 * q1, w11 * g1, att1)
    mine = [jnp.where(first, a, b) for a, b in zip(of_frame0, of_frame1)]
    out_ref[...] = jnp.concatenate(mine, axis=1).astype(BF16)
    theirs = jnp.where(first, att1, v0)
    att_ref[...] = jnp.concatenate([mine[3], theirs], axis=0).astype(BF16)


def term_kernel(parts, index_ref, att_ref, *refs):
    upstream = jnp.concatenate([ref[...] for ref in refs[:parts]], axis=0)
    mine_ref, theirs_ref = refs[parts:]
    att = mm(att_ref[...], expander(index_ref[...])).astype(BF16)
    half = mine_ref.shape[0]
    term = mm_tn(att, upstream).astype(BF16)
    mine_ref[...] = term[:half]
    theirs_ref[...] = term[half:]


def middle_back_kernel(
    order_ref, up_ref, mod_ref, middle_ref, rows_ref, weight, grad_ref
):
    middle = middle_ref[...]
    _, time, *_ = columns(middle.shape[1])
    back = behind(rows_ref[:, : 3 * WIDTH], weight, time, time + 3 * WIDTH, order_ref)
    gain = 1.0 + mod_ref[1:2, :]
    grad = up_ref[...].astype(F32) + norm_back(middle, gain, back)
    grad_ref[...] = grad


def result_kernel(slots, index_ref, middle_ref, rows_ref, weight, result_ref):
    att = mm(rows_ref[:, 3 * WIDTH :], expander(index_ref[2:3, :])).astype(BF16)
    *_, out, stop = columns(middle_ref.shape[1])
    grown = ahead(att, weight, out, stop, slots)
    result_ref[...] = (middle_ref[...] + grown).astype(BF16)


def space_back_kernel(
    tiles, place, pattern, q_ref, kv_ref, att_grad_ref, dq_ref, own_ref, low_ref, high_ref
):
    span = low_ref.shape[0]
    keys, values = kv_ref[:, :WIDTH], kv_ref[:, WIDTH:]
    allowed = space_allowed(place, pattern, span, tiles)
    spread_q = spread(q_ref[...])
    probs = softmax_of(spread_q, keys, allowed)
    dquery, dkeys, dvalues = attention_back(spread_q, keys, values, probs, att_grad_ref[...])
    dq_ref[...] = dquery.astype(BF16)
    both = jnp.concatenate([dkeys, dvalues], axis=1)
    low_ref[...] = both[:span].astype(BF16)
    own_ref[...] = both[span : 3 * span]
    high_ref[...] = both[3 * span :].astype(BF16)


def start_back_kernel(
    order_ref, x_ref, mod_ref, grad_ref, dq_ref, own_ref, left, right, weight, out_ref
):
    x = x_ref[...].astype(F32)
    rim = jnp.concatenate([left[...], right[...]], axis=0).astype(F32)
    dkv = own_ref[...] + rim
    grads = jnp.concatenate([dq_ref[...].astype(F32), dkv], axis=1).astype(BF16)
    back = behind(grads, weight, 0, 3 * WIDTH, order_ref)
    gain = 1.0 + mod_ref[0:1, :]
    out_ref[...] = (grad_ref[...] + norm_back(x, gain, back)).astype(BF16)


VMEM = pl.BlockSpec(memory_space=pltpu.VMEM)
SMEM = pl.BlockSpec(memory_space=pltpu.SMEM)


HBM = pl.BlockSpec(memory_space=pltpu.HBM)


def call(kernel, name, scalars, arrays, weight, outs, scratch=(), far=(), grant=VMEM_LIMIT):
    plain = len(scalars) + len(arrays) + len(far)
    weight, tree = jax.tree.flatten(list(weight))

    def body(*refs):
        fixed, pieces = refs[:plain], refs[plain : plain + len(weight)]
        pieces = (jax.tree.unflatten(tree, pieces),) if pieces else ()
        kernel(*fixed, *pieces, *refs[plain + len(weight) :])

    outs = [jax.ShapeDtypeStruct(shape, kind) for shape, kind in outs]
    near = [pltpu.VMEM(array.shape, array.dtype) for array in far]
    if far:
        near.append(pltpu.SemaphoreType.DMA((len(far),)))
    specs = [SMEM] * len(scalars) + [VMEM] * len(arrays) + [HBM] * len(far) + [VMEM] * len(weight)
    return pl.pallas_call(
        body,
        name=name,
        in_specs=specs,
        out_specs=[VMEM] * len(outs),
        out_shape=outs,
        scratch_shapes=near + list(scratch),
        compiler_params=pltpu.CompilerParams(vmem_limit_bytes=grant),
    )(*scalars, *arrays, *far, *weight)


def swapped(array, axis, bit):
    count = lax.axis_size(axis)
    return lax.ppermute(array, axis, [(i, i ^ bit) for i in range(count)])


def added(a, b):
    return (a.astype(F32) + b.astype(F32)).astype(BF16)


def relative_rows(shard, tile_at, clip_at, tiles, clips):
    block, inner = np.arange(clips * tiles * shard) // shard, np.arange(clips * tiles * shard) % shard
    low, apart, high = block // (2 * clips), block // 2 % clips, block % 2
    tile, clip = tile_at ^ (low + 2 * high), (clip_at + clips - apart) % clips
    return (clip * tiles + tile) * shard + inner


def local(
    latents,
    upstream,
    modulation,
    space_qkv,
    space_out,
    time_qkv,
    time_out,
    space_pattern,
    time_mask,
):
    seq, tiles, clips = lax.axis_size("seq"), lax.axis_size("tile"), lax.axis_size("dp")
    own, model = latents.shape[2], latents.shape[3]
    span, half = own // 2, own // 2
    shard = space_out.shape[0]
    x = latents.reshape(own, model)
    up = upstream.reshape(own, model)
    mod = modulation.reshape(modulation.shape[1:])
    tile_at, seq_at, clip_at = lax.axis_index("tile"), lax.axis_index("seq"), lax.axis_index("dp")
    side = seq_at if seq == 2 else jnp.zeros((), jnp.int32)
    place = jnp.stack([tile_at, side]).astype(jnp.int32)

    square = seq == 2 and tiles == 4
    hold = lax.optimization_barrier
    apart = range(1, clips)
    width = 6 * WIDTH + model
    own_w, half_w = call(
        pack_kernel, "pack", (), (), (),
        (((2 * shard, width), BF16), ((2 * shard, width // 2), BF16)),
        far=(space_qkv, time_qkv, space_out, time_out), grant=PACK_LIMIT,
    )
    if square:
        order = relative_rows(2 * shard, tile_at, clip_at, tiles, clips)
    else:
        order = jnp.arange(model)

    inner = order // (2 * shard) * shard + order % shard
    later = order % (2 * shard) >= shard
    space_rows = jnp.where((order >= 0) & ~later, inner, -1)
    time_rows = jnp.where((order >= 0) & later, inner, -1)
    index = jnp.stack([order, space_rows, time_rows]).astype(jnp.int32)
    near = np.arange(WIDTH) // shard
    bits = tiles.bit_length() - 1
    first = near // clips
    rel_tile = sum(((first >> b) & 1) << (bits - 1 - b) for b in range(bits))
    owner = (clip_at ^ (near % clips)) * tiles + (tile_at ^ rel_tile)
    terms = (owner * shard + np.arange(WIDTH) % shard).astype(jnp.int32).reshape(1, WIDTH)

    rise = [(i, i + 1) for i in range(tiles - 1)]
    fall = [(i + 1, i) for i in range(tiles - 1)]

    def rims(rows):
        before = lax.ppermute(rows[span:], "tile", rise)
        return before, lax.ppermute(rows[:span], "tile", fall)

    def joined(owned, pieces):
        rows = owned * 2 * shard + (4 * shard if len(pieces) > owned else 0)
        return call(
            functools.partial(join_kernel, owned), "join", (place,), pieces, (),
            (((rows, columns(model)[-1]), BF16),),
        )[0]

    (made,) = call(order_kernel, "order", (), (index,), (), (((model, model), BF16),))

    def normed_of(order, before, rows, after):
        return call(
            normed_kernel, "normed", (), (order, before, rows, after, mod), (),
            (((2 * own, model), BF16),),
        )[0]

    if square:
        lanes = width // 2
        cut = lanes // 256 * 128

        def onward(piece):
            return lax.ppermute(piece, "dp", [(i, (i + 1) % clips) for i in range(clips)])

        def sends(piece, by_tile, by_seq, owned=(), parts=()):
            arrays = [by_tile, by_seq] if piece is None else [piece, by_tile, by_seq]
            at, count, joins = (0 if piece is None else lanes), len(arrays), len(owned) + len(parts)

            def kernel(place_ref, *refs):
                sides, earlier, outs = refs[:count], refs[count : count + joins], refs[count + joins :]
                sides = sides if piece is not None else (None,) + sides
                send_kernel((cut, lanes), *sides, *outs[:2])
                if joins:
                    join_kernel(len(owned), place_ref, *earlier, outs[2])

            outs = [((2 * shard, at + cut), BF16), ((2 * shard, at + lanes - cut), BF16)]
            if joins:
                rows = len(owned) * 2 * shard + 4 * shard
                outs.append(((rows, columns(model)[-1]), BF16))
            over_tile, over_seq, *group = call(
                kernel, "send", (place,), (*arrays, *owned, *parts), (), outs
            )
            return group, (swapped(over_tile, "tile", 2), swapped(over_seq, "seq", 1))

        across = swapped(own_w, "tile", 2)
        piece, other_x, early = hold((onward(half_w), swapped(x, "seq", 1), x))
        pieces, came, groups, others = [piece], [], [], []
        for step in range(clips):
            piece = pieces[step] if step < clips - 1 else None
            following = onward(piece) if step < clips - 2 else ()
            if step == 0:
                moves = swapped(piece, "tile", 2), swapped(piece, "seq", 1)
                moves, across = hold((moves, across))
            else:
                owned = [own_w, across] if step == 2 else []
                parts = [pieces[step - 2], *came[step - 2], *came[step - 1]] if step > 1 else []
                group, moves = sends(piece, *came[-1], owned, parts)
                if group:
                    groups += group
                    others.append(swapped(groups[-1], "tile", 1))
            if step == 1:
                moves, made = hold((moves, made))
            if step == clips - 1:
                early, *_ = hold((early, came[-1]))
                before, after = rims(early)
            moves, following, others = hold((moves, following, others))
            came.append(moves)
            if step < clips - 2:
                pieces.append(following)
        order = made
        late_up, _ = hold((up, came[-1]))
        other_up = swapped(late_up, "seq", 1)
        last, before, after = hold(
            (joined(0, [pieces[-1], *came[-2], *came[-1]]), before, after)
        )
        groups.append(last)
        others.append(swapped(groups[-1], "tile", 1))
        normed = normed_of(order, before, x, after)
        weight = groups + others
        late = [len(groups) - 1, len(weight) - 1]
    else:
        before, after = rims(x)
        order = made
        normed = normed_of(order, before, x, after)
        weight = [lax.all_gather(joined(1, [own_w]), ("dp", "tile"), axis=0, tiled=True)]
        late = [0]
    ends = np.cumsum([0] + [part.shape[0] for part in weight]).tolist()
    slots = [(at, part.shape[0]) for at, part in zip(ends, weight)]
    first = [n for n in range(len(weight)) if n not in late]
    partial = ()
    if first:
        partial = tuple(call(
            functools.partial(early_kernel, [slots[n] for n in first]), "space_early", (),
            (normed,), [weight[n] for n in first], (((2 * own, 3 * WIDTH), F32),),
        ))

    query, window, att = call(
        functools.partial(forward_kernel, tiles, slots, late), "forward", (place, space_pattern),
        (normed,) + partial, weight,
        (((own, WIDTH), BF16), ((2 * own, 2 * WIDTH), BF16), ((own, WIDTH), BF16)),
    )
    middle, rows = call(
        functools.partial(middle_kernel, slots), "middle", (), (index, order, x, mod, att), weight,
        (((own, model), F32), ((own, 3 * WIDTH), BF16)),
    )
    if square:
        att, other_up = hold((att, other_up))
        ups = (up, other_up)
        other_att = swapped(att, "seq", 1)
    else:
        def turned(array):
            parts = array.reshape(seq, own // seq, array.shape[1])
            parts = lax.all_to_all(parts, "seq", split_axis=0, concat_axis=0, tiled=True)
            return parts.reshape(array.shape)

        ups = (turned(up),)
    (time_att_grad,) = call(
        functools.partial(att_grad_kernel, len(ups), 2), "att_grad", (), (index,) + ups, weight,
        (((len(ups) * own, WIDTH), BF16),),
    )
    if square:
        rows, att = call(
            functools.partial(time_pair_kernel, slots), "time_att", (place, time_mask),
            (index, order, mod, other_x, other_att, rows, time_att_grad), weight,
            (((own, 4 * WIDTH), BF16), ((2 * own, WIDTH), BF16)),
        )
    else:
        token = jnp.arange(own)
        frame, patch = token // (own // seq), token % (own // seq)
        seen = jnp.take(jnp.take(time_mask, frame, axis=0), frame, axis=1) == 1
        seen = (seen & (frame[None, :] < frame[:, None])) | (frame[None, :] == frame[:, None])
        allowed = (seen & (patch[None, :] == patch[:, None])).astype(jnp.int32)
        (rows,) = call(
            time_att_kernel, "time_att", (), (allowed, turned(rows), time_att_grad), (),
            (((own, 4 * WIDTH), BF16),),
        )
        att = rows[:, 3 * WIDTH :]
        rows = turned(rows)
    mine, theirs = call(
        functools.partial(term_kernel, len(ups)), "term", (), (terms, att) + ups, (),
        (((WIDTH // 2, model), BF16),) * 2,
    )

    (grad,) = call(
        middle_back_kernel, "middle_back", (), (order, up, mod, middle, rows), weight,
        (((own, model), F32),),
    )
    (att_grad,) = call(
        functools.partial(att_grad_kernel, 1, 1), "space_grad", (), (index, grad), weight,
        (((own, WIDTH), BF16),),
    )
    dq, own_grads, to_left, to_right = call(
        functools.partial(space_back_kernel, tiles), "space_back", (place, space_pattern),
        (query, window, att_grad), (),
        (
            ((own, WIDTH), BF16), ((own, 2 * WIDTH), F32),
            ((span, 2 * WIDTH), BF16), ((span, 2 * WIDTH), BF16),
        ),
    )
    from_left = lax.ppermute(to_right, "tile", rise)
    from_right = lax.ppermute(to_left, "tile", fall)
    (start_grad,) = call(
        start_back_kernel, "start_back", (),
        (order, x, mod, grad, dq, own_grads, from_left, from_right), weight,
        (((own, model), BF16),),
    )
    late, _ = hold((rows, start_grad))
    (result,) = call(
        functools.partial(result_kernel, slots), "result", (),
        (index, middle, late), weight, (((own, model), BF16),),
    )

    def ended(came, kernel):
        return hold((came, kernel))[0]

    ends, bit = [grad], 1
    while bit < tiles:
        came = ended(swapped(theirs, "tile", bit), ends.pop(0) if ends else dq)
        mine = added(mine, came)
        bit *= 2
        if bit < tiles:
            rows = mine.shape[0] // 2
            mine, theirs = mine[:rows], mine[rows:]
    came = [swapped(mine[by * shard : (by + 1) * shard], "dp", by) for by in apart]
    came = ended(came, result)
    total = mine[:shard].astype(F32)
    for part in came:
        total = total + part.astype(F32)
    if not square:
        total = lax.psum(total.astype(BF16), "seq").astype(F32)
    return (result.reshape(latents.shape), start_grad.reshape(latents.shape), total)


def solution(mesh):
    in_specs = (
        P("dp", "seq", "tile", None),
        P("dp", "seq", "tile", None),
        P("dp", None, None),
        P(("dp", "tile"), None),
        P(("dp", "tile"), None),
        P(("dp", "tile"), None),
        P(("dp", "tile"), None),
        P("tile", None),
        P(),
    )
    out_specs = (
        P("dp", "seq", "tile", None),
        P("dp", "seq", "tile", None),
        P(("dp", "tile"), None),
    )
    return jax.shard_map(local, mesh=mesh, in_specs=in_specs, out_specs=out_specs, check_vma=False)
```

```python
import functools

import jax
import jax.numpy as jnp
import numpy as np
from jax import lax
from jax.experimental import pallas as pl
from jax.experimental.pallas import tpu as pltpu
from jax.sharding import PartitionSpec as P

HEADS = 8
HEAD_DIM = 72
WIDTH = HEADS * HEAD_DIM
EPSILON = 1e-06
MASKED = -1e30
SCALE = HEAD_DIM ** (-0.5)
BF16 = jnp.bfloat16
F32 = jnp.float32
VMEM_LIMIT = 16 * 1024 * 1024
PACK_LIMIT = 63 * 1024 * 1024
SHORT = pl.CostEstimate(flops=1024, bytes_accessed=1024, transcendentals=0)


def mm(a, b):
    return jnp.dot(a, b, preferred_element_type=F32)


def mm_nt(a, b):
    return lax.dot_general(a, b, (((1,), (1,)), ((), ())), preferred_element_type=F32)


def mm_tn(a, b):
    return lax.dot_general(a, b, (((0,), (0,)), ((), ())), preferred_element_type=F32)


def head_masks(kind):
    lane = lax.broadcasted_iota(jnp.int32, (1, WIDTH), 1)
    inside = [(lane >= HEAD_DIM * h) & (lane < HEAD_DIM * (h + 1)) for h in range(HEADS)]
    return [jnp.where(hit, 1.0, 0.0).astype(kind) for hit in inside]


def spread(rows):
    return jnp.concatenate([rows * mask for mask in head_masks(rows.dtype)], axis=0)


def collect(big):
    n = big.shape[0] // HEADS
    masks = head_masks(F32)
    total = big[:n] * masks[0]
    for h in range(1, HEADS):
        total = total + big[h * n : (h + 1) * n] * masks[h]
    return total


def softmax_of(spread_q, keys, allowed):
    n, m = allowed.shape
    scores = (mm_nt(spread_q, keys) * SCALE).reshape(HEADS, n, m)
    scores = jnp.where((allowed > 0)[None], scores, MASKED)
    raised = jnp.exp(scores - jnp.max(scores, axis=-1, keepdims=True))
    probs = raised / jnp.sum(raised, axis=-1, keepdims=True)
    return probs.reshape(HEADS * n, m)


def attention_back(spread_q, keys, values, probs, grad):
    spread_g = spread(grad)
    dprob = mm_nt(spread_g, values)
    delta = jnp.sum(probs * dprob, axis=-1, keepdims=True)
    dscore = (probs * (dprob - delta) * SCALE).astype(BF16)
    dquery = collect(mm(dscore, keys))
    dkeys = mm_tn(dscore, spread_q)
    dvalues = mm_tn(probs.astype(BF16), spread_g)
    return dquery, dkeys, dvalues


def inverse_of(values):
    return lax.rsqrt(jnp.mean(values * values, axis=-1, keepdims=True) + EPSILON)


def norm_back(values, gain, grad):
    inverse = inverse_of(values)
    scaled = grad * gain
    cubed = inverse * inverse * inverse
    return inverse * scaled - values * cubed * jnp.mean(scaled * values, axis=-1, keepdims=True)


def expander(source, rows=WIDTH):
    row = lax.broadcasted_iota(jnp.int32, (rows, source.shape[1]), 0)
    return jnp.where(row == source, 1.0, 0.0).astype(BF16)


def ahead(rows, weight, start, stop, slots):
    total = None
    for (at, count), ref in zip(slots, weight):
        term = mm(rows[:, at : at + count], ref[:, start:stop])
        total = term if total is None else total + term
    return total


def behind(grad, weight, start, stop, select, rounded=False):
    count = grad.shape[0]
    turned = grad.astype(F32).T.astype(BF16)
    parts = [mm(ref[:, start:stop], turned) for ref in weight]
    part = jnp.concatenate(parts, axis=0)
    high = part.astype(BF16)
    if rounded:
        return mm(select[...], high).T.astype(BF16)
    low = (part - high.astype(F32)).astype(BF16)
    both = mm(select[...], jnp.concatenate([high, low], axis=1))
    return (both[:, :count] + both[:, count:]).T


def space_allowed(place, pattern, span, tiles):
    own = 2 * span
    row = lax.broadcasted_iota(jnp.int32, (own, 4 * span), 0)
    column = lax.broadcasted_iota(jnp.int32, (own, 4 * span), 1)
    tile_at = place[0]
    allowed = jnp.zeros((own, 4 * span), jnp.int32)
    for b in range(2):
        for r in range(4):
            block = 2 * tile_at - 1 + r
            inside = (block >= 0) & (block < 2 * tiles)
            seen = inside if r == b + 1 else inside & (pattern[b, r] == 1)
            here = (row >= b * span) & (row < (b + 1) * span)
            here = here & (column >= r * span) & (column < (r + 1) * span)
            allowed = allowed + jnp.where(here, seen.astype(jnp.int32), 0)
    return allowed


def fetch(sources, buffers, semaphores):
    copies = [
        pltpu.make_async_copy(source, buffer, semaphores.at[number])
        for number, (source, buffer) in enumerate(zip(sources, buffers))
    ]
    for copy in copies:
        copy.start()
    for copy in copies:
        copy.wait()


def columns(model):
    wide = -(-3 * WIDTH // 128) * 128
    return 0, wide, 2 * wide, 2 * wide + model


def pack_kernel(
    space_hbm, time_hbm, space_out_hbm, time_out_hbm, packed, half_ref,
    space_qkv, time_qkv, space_out, time_out, ready,
):
    fetch(
        (space_hbm, time_hbm, space_out_hbm, time_out_hbm),
        (space_qkv, time_qkv, space_out, time_out), ready,
    )
    outs = jnp.concatenate([space_out[...].astype(F32), time_out[...].astype(F32)], axis=0)
    parts = [space_qkv[...].astype(F32), time_qkv[...].astype(F32), outs]
    packed[...] = jnp.concatenate(parts, axis=1).astype(BF16)
    lanes = half_ref.shape[1]
    first = lax.axis_index("seq") == 0

    @pl.when(first)
    def _():
        half_ref[...] = packed[:, :lanes]

    @pl.when(jnp.logical_not(first))
    def _():
        half_ref[...] = packed[:, lanes:]


def send_kernel(cut, piece, by_tile, by_seq, over_tile, over_seq):
    at, lanes = 0, cut[1]
    if piece is not None:
        at = piece.shape[1]
        over_tile[:, :at] = piece[...]
        over_seq[:, :at] = piece[...]
    over_tile[:, at:] = by_seq[:, : cut[0]]
    over_seq[:, at:] = by_tile[:, cut[0] : lanes]


def place_columns(out_ref, row, full):
    rows = slice(row, row + full.shape[0])
    space, time, out, stop = columns(full.shape[1] - 6 * WIDTH)
    pad = jnp.zeros((full.shape[0], time - space - 3 * WIDTH), BF16)
    out_ref[rows, space : space + 3 * WIDTH] = full[:, : 3 * WIDTH].astype(BF16)
    out_ref[rows, space + 3 * WIDTH : time] = pad
    out_ref[rows, time : time + 3 * WIDTH] = full[:, 3 * WIDTH : 6 * WIDTH].astype(BF16)
    out_ref[rows, time + 3 * WIDTH : out] = pad
    out_ref[rows, out:stop] = full[:, 6 * WIDTH :].astype(BF16)


def join_kernel(owned, place, *refs):
    whole, parts, out_ref = refs[:owned], refs[owned:-1], refs[-1]
    top = 0
    if whole:
        rows = [ref[...].astype(F32) for ref in whole]
        place_columns(out_ref, 0, jnp.concatenate(rows, axis=0))
        top = sum(ref.shape[0] for ref in whole)
    if not parts:
        return
    near, by_tile, by_seq, corner_low, corner_high = parts
    lanes = near.shape[1]
    mine = [near[...].astype(F32), by_tile[:, :lanes].astype(F32)]
    mine = jnp.concatenate(mine, axis=0)
    low, high = corner_low.shape[1] % lanes, corner_high.shape[1] % lanes
    corner = [
        corner_low[:, corner_low.shape[1] - low :].astype(F32),
        corner_high[:, corner_high.shape[1] - high :].astype(F32),
    ]
    corner = jnp.concatenate(corner, axis=1)
    other = jnp.concatenate([by_seq[:, :lanes].astype(F32), corner], axis=0)

    @pl.when(place[1] == 0)
    def _():
        place_columns(out_ref, top, jnp.concatenate([mine, other], axis=1))

    @pl.when(place[1] != 0)
    def _():
        place_columns(out_ref, top, jnp.concatenate([other, mine], axis=1))


def order_kernel(index_ref, order_ref):
    order_ref[...] = expander(index_ref[0:1, :], order_ref.shape[0])


def normed_kernel(order_ref, before, x_ref, after, mod_ref, normed_ref):
    x = jnp.concatenate([before[...], x_ref[...], after[...]], axis=0).astype(F32)
    normed = (x * inverse_of(x) * (1.0 + mod_ref[0:1, :])).astype(BF16)
    normed_ref[...] = mm(normed, order_ref[...]).astype(BF16)


def early_kernel(slots, normed_ref, weight, partial_ref):
    partial_ref[...] = ahead(normed_ref, weight, 0, 3 * WIDTH, slots)


def forward_kernel(tiles, slots, late, place, pattern, normed_ref, *refs):
    *partial, weight, q_ref, kv_ref, att_ref = refs
    own = q_ref.shape[0]
    span = own // 2
    rows = ahead(
        normed_ref, [weight[n] for n in late], 0, 3 * WIDTH, [slots[n] for n in late]
    )
    for earlier in partial:
        rows = rows + earlier[...]
    rows = rows.astype(BF16)
    query, kv = rows[span : span + own, :WIDTH], rows[:, WIDTH:]
    keys, values = kv[:, :WIDTH], kv[:, WIDTH:]
    q_ref[...] = query
    kv_ref[...] = kv
    allowed = space_allowed(place, pattern, span, tiles)
    probs = softmax_of(spread(query), keys, allowed)
    att_ref[...] = collect(mm(probs.astype(BF16), values)).astype(BF16)


def middle_of(slots, index_ref, order_ref, x_ref, mod_ref, att, weight):
    _, time, out, stop = columns(x_ref.shape[1])
    att = mm(att, expander(index_ref[1:2, :])).astype(BF16)
    middle = x_ref[...].astype(F32) + ahead(att, weight, out, stop, slots)
    normed = (middle * inverse_of(middle) * (1.0 + mod_ref[1:2, :])).astype(BF16)
    normed = mm(normed, order_ref[...]).astype(BF16)
    return middle, ahead(normed, weight, time, time + 3 * WIDTH, slots).astype(BF16)


def middle_kernel(slots, index_ref, order_ref, x_ref, mod_ref, att_ref, weight, middle_ref, rows_ref):
    middle, rows = middle_of(slots, index_ref, order_ref, x_ref, mod_ref, att_ref[...], weight)
    middle_ref[...] = middle
    rows_ref[...] = rows


def att_grad_kernel(parts, row, index_ref, *refs):
    upstream = jnp.concatenate([ref[...] for ref in refs[:parts]], axis=0).astype(BF16)
    weight, grad_ref = refs[parts:]
    *_, out, stop = columns(upstream.shape[1])
    grad_ref[...] = behind(
        upstream, weight, out, stop, expander(index_ref[row : row + 1, :]), rounded=True
    )


def time_att_kernel(allowed_ref, rows_ref, grad_ref, out_ref):
    rows = rows_ref[...]
    query, keys, values = rows[:, :WIDTH], rows[:, WIDTH : 2 * WIDTH], rows[:, 2 * WIDTH :]
    spread_q = spread(query)
    probs = softmax_of(spread_q, keys, allowed_ref[...])
    att = collect(mm(probs.astype(BF16), values))
    grads = attention_back(spread_q, keys, values, probs, grad_ref[...])
    out_ref[...] = jnp.concatenate(grads + (att,), axis=1).astype(BF16)


def time_pair_kernel(
    slots, place, time_mask, index_ref, order_ref, mod_ref, x_ref, space_ref, own_ref, grad_ref,
    weight, out_ref, att_ref,
):
    count = own_ref.shape[0]
    first = place[1] == 0

    def frames(own, other):
        own, other = own.astype(F32), other.astype(F32)
        return jnp.where(first, own, other), jnp.where(first, other, own)

    _, other = middle_of(slots, index_ref, order_ref, x_ref, mod_ref, space_ref[...], weight)
    own = own_ref[...]
    row = lax.broadcasted_iota(jnp.int32, (WIDTH, 128), 0)
    low = lax.broadcasted_iota(jnp.int32, (WIDTH, 128), 1) * HEAD_DIM
    heads = jnp.where((row >= low) & (row < low + HEAD_DIM), 1.0, 0.0).astype(BF16)

    def summed(product):
        high = product.astype(BF16)
        return mm(high, heads) + mm((product - high.astype(F32)).astype(BF16), heads)

    def widened(value):
        return mm_nt(value.astype(BF16), heads)

    _, q1 = frames(own[:, :WIDTH], other[:, :WIDTH])
    k0, k1 = frames(own[:, WIDTH : 2 * WIDTH], other[:, WIDTH : 2 * WIDTH])
    v0, v1 = frames(own[:, 2 * WIDTH :], other[:, 2 * WIDTH :])
    g0, g1 = frames(grad_ref[:count, :], grad_ref[count:, :])
    s10 = jnp.where(time_mask[1, 0] == 1, summed(q1 * k0) * SCALE, MASKED)
    s11 = summed(q1 * k1) * SCALE
    top = jnp.maximum(s10, s11)
    e10, e11 = jnp.exp(s10 - top), jnp.exp(s11 - top)
    total = e10 + e11
    p10, p11 = e10 / total, e11 / total
    dp10, dp11 = summed(g1 * v0), summed(g1 * v1)
    delta = p10 * dp10 + p11 * dp11
    d10, d11 = widened(p10 * (dp10 - delta) * SCALE), widened(p11 * (dp11 - delta) * SCALE)
    w10, w11 = widened(p10), widened(p11)
    att1 = w10 * v0 + w11 * v1
    zero = jnp.zeros_like(q1)
    of_frame0 = (zero, d10 * q1, g0 + w10 * g1, v0)
    of_frame1 = (d10 * k0 + d11 * k1, d11 * q1, w11 * g1, att1)
    mine = [jnp.where(first, a, b) for a, b in zip(of_frame0, of_frame1)]
    out_ref[...] = jnp.concatenate(mine, axis=1).astype(BF16)
    theirs = jnp.where(first, att1, v0)
    att_ref[...] = jnp.concatenate([mine[3], theirs], axis=0).astype(BF16)


def term_kernel(parts, index_ref, att_ref, *refs):
    upstream = jnp.concatenate([ref[...] for ref in refs[:parts]], axis=0)
    mine_ref, theirs_ref = refs[parts:]
    att = mm(att_ref[...], expander(index_ref[...])).astype(BF16)
    half = mine_ref.shape[0]
    term = mm_tn(att, upstream).astype(BF16)
    mine_ref[...] = term[:half]
    theirs_ref[...] = term[half:]


def middle_back_kernel(
    order_ref, up_ref, mod_ref, middle_ref, rows_ref, weight, grad_ref
):
    middle = middle_ref[...]
    _, time, *_ = columns(middle.shape[1])
    back = behind(rows_ref[:, : 3 * WIDTH], weight, time, time + 3 * WIDTH, order_ref)
    gain = 1.0 + mod_ref[1:2, :]
    grad = up_ref[...].astype(F32) + norm_back(middle, gain, back)
    grad_ref[...] = grad


def result_kernel(slots, index_ref, middle_ref, rows_ref, weight, result_ref):
    att = mm(rows_ref[:, 3 * WIDTH :], expander(index_ref[2:3, :])).astype(BF16)
    *_, out, stop = columns(middle_ref.shape[1])
    grown = ahead(att, weight, out, stop, slots)
    result_ref[...] = (middle_ref[...] + grown).astype(BF16)


def space_back_kernel(
    tiles, place, pattern, q_ref, kv_ref, att_grad_ref, dq_ref, own_ref, low_ref, high_ref
):
    span = low_ref.shape[0]
    keys, values = kv_ref[:, :WIDTH], kv_ref[:, WIDTH:]
    allowed = space_allowed(place, pattern, span, tiles)
    spread_q = spread(q_ref[...])
    probs = softmax_of(spread_q, keys, allowed)
    dquery, dkeys, dvalues = attention_back(spread_q, keys, values, probs, att_grad_ref[...])
    dq_ref[...] = dquery.astype(BF16)
    both = jnp.concatenate([dkeys, dvalues], axis=1)
    low_ref[...] = both[:span].astype(BF16)
    own_ref[...] = both[span : 3 * span]
    high_ref[...] = both[3 * span :].astype(BF16)


def start_back_kernel(
    order_ref, x_ref, mod_ref, grad_ref, dq_ref, own_ref, left, right, weight, out_ref
):
    x = x_ref[...].astype(F32)
    rim = jnp.concatenate([left[...], right[...]], axis=0).astype(F32)
    dkv = own_ref[...] + rim
    grads = jnp.concatenate([dq_ref[...].astype(F32), dkv], axis=1).astype(BF16)
    back = behind(grads, weight, 0, 3 * WIDTH, order_ref)
    gain = 1.0 + mod_ref[0:1, :]
    out_ref[...] = (grad_ref[...] + norm_back(x, gain, back)).astype(BF16)


VMEM = pl.BlockSpec(memory_space=pltpu.VMEM)
SMEM = pl.BlockSpec(memory_space=pltpu.SMEM)


HBM = pl.BlockSpec(memory_space=pltpu.HBM)


def call(kernel, name, scalars, arrays, weight, outs, scratch=(), far=(), grant=VMEM_LIMIT, cost=None):
    plain = len(scalars) + len(arrays) + len(far)
    weight, tree = jax.tree.flatten(list(weight))

    def body(*refs):
        fixed, pieces = refs[:plain], refs[plain : plain + len(weight)]
        pieces = (jax.tree.unflatten(tree, pieces),) if pieces else ()
        kernel(*fixed, *pieces, *refs[plain + len(weight) :])

    outs = [jax.ShapeDtypeStruct(shape, kind) for shape, kind in outs]
    near = [pltpu.VMEM(array.shape, array.dtype) for array in far]
    if far:
        near.append(pltpu.SemaphoreType.DMA((len(far),)))
    specs = [SMEM] * len(scalars) + [VMEM] * len(arrays) + [HBM] * len(far) + [VMEM] * len(weight)
    return pl.pallas_call(
        body,
        name=name,
        in_specs=specs,
        out_specs=[VMEM] * len(outs),
        out_shape=outs,
        scratch_shapes=near + list(scratch),
        compiler_params=pltpu.CompilerParams(vmem_limit_bytes=grant),
        cost_estimate=cost,
    )(*scalars, *arrays, *far, *weight)


def swapped(array, axis, bit):
    count = lax.axis_size(axis)
    return lax.ppermute(array, axis, [(i, i ^ bit) for i in range(count)])


def added(a, b):
    return (a.astype(F32) + b.astype(F32)).astype(BF16)


def relative_rows(shard, tile_at, clip_at, tiles, clips):
    block, inner = np.arange(clips * tiles * shard) // shard, np.arange(clips * tiles * shard) % shard
    low, apart, high = block // (2 * clips), block // 2 % clips, block % 2
    tile, clip = tile_at ^ (low + 2 * high), (clip_at + clips - apart) % clips
    return (clip * tiles + tile) * shard + inner


def local(
    latents,
    upstream,
    modulation,
    space_qkv,
    space_out,
    time_qkv,
    time_out,
    space_pattern,
    time_mask,
):
    seq, tiles, clips = lax.axis_size("seq"), lax.axis_size("tile"), lax.axis_size("dp")
    own, model = latents.shape[2], latents.shape[3]
    span, half = own // 2, own // 2
    shard = space_out.shape[0]
    x = latents.reshape(own, model)
    up = upstream.reshape(own, model)
    mod = modulation.reshape(modulation.shape[1:])
    tile_at, seq_at, clip_at = lax.axis_index("tile"), lax.axis_index("seq"), lax.axis_index("dp")
    side = seq_at if seq == 2 else jnp.zeros((), jnp.int32)
    place = jnp.stack([tile_at, side]).astype(jnp.int32)

    square = seq == 2 and tiles == 4
    hold = lax.optimization_barrier
    apart = range(1, clips)
    width = 6 * WIDTH + model
    own_w, half_w = call(
        pack_kernel, "pack", (), (), (),
        (((2 * shard, width), BF16), ((2 * shard, width // 2), BF16)),
        far=(space_qkv, time_qkv, space_out, time_out), grant=PACK_LIMIT,
    )
    if square:
        order = relative_rows(2 * shard, tile_at, clip_at, tiles, clips)
    else:
        order = jnp.arange(model)

    inner = order // (2 * shard) * shard + order % shard
    later = order % (2 * shard) >= shard
    space_rows = jnp.where((order >= 0) & ~later, inner, -1)
    time_rows = jnp.where((order >= 0) & later, inner, -1)
    index = jnp.stack([order, space_rows, time_rows]).astype(jnp.int32)
    near = np.arange(WIDTH) // shard
    bits = tiles.bit_length() - 1
    first = near // clips
    rel_tile = sum(((first >> b) & 1) << (bits - 1 - b) for b in range(bits))
    owner = (clip_at ^ (near % clips)) * tiles + (tile_at ^ rel_tile)
    terms = (owner * shard + np.arange(WIDTH) % shard).astype(jnp.int32).reshape(1, WIDTH)

    rise = [(i, i + 1) for i in range(tiles - 1)]
    fall = [(i + 1, i) for i in range(tiles - 1)]

    def rims(rows):
        before = lax.ppermute(rows[span:], "tile", rise)
        return before, lax.ppermute(rows[:span], "tile", fall)

    def joined(owned, pieces):
        rows = owned * 2 * shard + (4 * shard if len(pieces) > owned else 0)
        return call(
            functools.partial(join_kernel, owned), "join", (place,), pieces, (),
            (((rows, columns(model)[-1]), BF16),),
        )[0]

    (made,) = call(order_kernel, "order", (), (index,), (), (((model, model), BF16),))

    def normed_of(order, before, rows, after):
        return call(
            normed_kernel, "normed", (), (order, before, rows, after, mod), (),
            (((2 * own, model), BF16),),
        )[0]

    if square:
        lanes = width // 2
        cut = lanes // 256 * 128

        def onward(piece):
            return lax.ppermute(piece, "dp", [(i, (i + 1) % clips) for i in range(clips)])

        def sends(piece, by_tile, by_seq, owned=(), parts=()):
            arrays = [by_tile, by_seq] if piece is None else [piece, by_tile, by_seq]
            at, count, joins = (0 if piece is None else lanes), len(arrays), len(owned) + len(parts)

            def kernel(place_ref, *refs):
                sides, earlier, outs = refs[:count], refs[count : count + joins], refs[count + joins :]
                sides = sides if piece is not None else (None,) + sides
                send_kernel((cut, lanes), *sides, *outs[:2])
                if joins:
                    join_kernel(len(owned), place_ref, *earlier, outs[2])

            outs = [((2 * shard, at + cut), BF16), ((2 * shard, at + lanes - cut), BF16)]
            if joins:
                rows = len(owned) * 2 * shard + 4 * shard
                outs.append(((rows, columns(model)[-1]), BF16))
            over_tile, over_seq, *group = call(
                kernel, "send", (place,), (*arrays, *owned, *parts), (), outs
            )
            return group, (swapped(over_tile, "tile", 2), swapped(over_seq, "seq", 1))

        across = swapped(own_w, "tile", 2)
        piece, other_x, early = hold((onward(half_w), swapped(x, "seq", 1), x))
        pieces, came, groups, others = [piece], [], [], []
        for step in range(clips):
            piece = pieces[step] if step < clips - 1 else None
            following = onward(piece) if step < clips - 2 else ()
            if step == 0:
                moves = swapped(piece, "tile", 2), swapped(piece, "seq", 1)
                moves, across = hold((moves, across))
            else:
                owned = [own_w, across] if step == 2 else []
                parts = [pieces[step - 2], *came[step - 2], *came[step - 1]] if step > 1 else []
                group, moves = sends(piece, *came[-1], owned, parts)
                if group:
                    groups += group
                    others.append(swapped(groups[-1], "tile", 1))
            if step == 1:
                moves, made = hold((moves, made))
            if step == clips - 2:
                early, *_ = hold((early, came[-1]))
                moves, before, after = hold((moves, *rims(early)))
            if step == clips - 1:
                normed = normed_of(made, before, x, after)
                moves, normed = hold((moves, normed))
            moves, following, others = hold((moves, following, others))
            came.append(moves)
            if step < clips - 2:
                pieces.append(following)
        order = made
        late_up, _ = hold((up, came[-1]))
        other_up = swapped(late_up, "seq", 1)
        groups.append(joined(0, [pieces[-1], *came[-2], *came[-1]]))
        others.append(swapped(groups[-1], "tile", 1))
        weight = groups + others
        late = [len(groups) - 1, len(weight) - 1]
    else:
        before, after = rims(x)
        order = made
        normed = normed_of(order, before, x, after)
        weight = [lax.all_gather(joined(1, [own_w]), ("dp", "tile"), axis=0, tiled=True)]
        late = [0]
    ends = np.cumsum([0] + [part.shape[0] for part in weight]).tolist()
    slots = [(at, part.shape[0]) for at, part in zip(ends, weight)]
    first = [n for n in range(len(weight)) if n not in late]
    partial = ()
    if first:
        partial = tuple(call(
            functools.partial(early_kernel, [slots[n] for n in first]), "space_early", (),
            (normed,), [weight[n] for n in first], (((2 * own, 3 * WIDTH), F32),), cost=SHORT,
        ))

    query, window, att = call(
        functools.partial(forward_kernel, tiles, slots, late), "forward", (place, space_pattern),
        (normed,) + partial, weight,
        (((own, WIDTH), BF16), ((2 * own, 2 * WIDTH), BF16), ((own, WIDTH), BF16)), cost=SHORT,
    )
    middle, rows = call(
        functools.partial(middle_kernel, slots), "middle", (), (index, order, x, mod, att), weight,
        (((own, model), F32), ((own, 3 * WIDTH), BF16)),
    )
    if square:
        ups = (up, other_up)
        other_att = swapped(att, "seq", 1)
    else:
        def turned(array):
            parts = array.reshape(seq, own // seq, array.shape[1])
            parts = lax.all_to_all(parts, "seq", split_axis=0, concat_axis=0, tiled=True)
            return parts.reshape(array.shape)

        ups = (turned(up),)
    (time_att_grad,) = call(
        functools.partial(att_grad_kernel, len(ups), 2), "att_grad", (), (index,) + ups, weight,
        (((len(ups) * own, WIDTH), BF16),),
    )
    if square:
        rows, att = call(
            functools.partial(time_pair_kernel, slots), "time_att", (place, time_mask),
            (index, order, mod, other_x, other_att, rows, time_att_grad), weight,
            (((own, 4 * WIDTH), BF16), ((2 * own, WIDTH), BF16)),
        )
    else:
        token = jnp.arange(own)
        frame, patch = token // (own // seq), token % (own // seq)
        seen = jnp.take(jnp.take(time_mask, frame, axis=0), frame, axis=1) == 1
        seen = (seen & (frame[None, :] < frame[:, None])) | (frame[None, :] == frame[:, None])
        allowed = (seen & (patch[None, :] == patch[:, None])).astype(jnp.int32)
        (rows,) = call(
            time_att_kernel, "time_att", (), (allowed, turned(rows), time_att_grad), (),
            (((own, 4 * WIDTH), BF16),),
        )
        att = rows[:, 3 * WIDTH :]
        rows = turned(rows)
    mine, theirs = call(
        functools.partial(term_kernel, len(ups)), "term", (), (terms, att) + ups, (),
        (((WIDTH // 2, model), BF16),) * 2,
    )

    (grad,) = call(
        middle_back_kernel, "middle_back", (), (order, up, mod, middle, rows), weight,
        (((own, model), F32),),
    )
    (att_grad,) = call(
        functools.partial(att_grad_kernel, 1, 1), "space_grad", (), (index, grad), weight,
        (((own, WIDTH), BF16),),
    )
    dq, own_grads, to_left, to_right = call(
        functools.partial(space_back_kernel, tiles), "space_back", (place, space_pattern),
        (query, window, att_grad), (),
        (
            ((own, WIDTH), BF16), ((own, 2 * WIDTH), F32),
            ((span, 2 * WIDTH), BF16), ((span, 2 * WIDTH), BF16),
        ),
    )
    from_left = lax.ppermute(to_right, "tile", rise)
    from_right = lax.ppermute(to_left, "tile", fall)
    (start_grad,) = call(
        start_back_kernel, "start_back", (),
        (order, x, mod, grad, dq, own_grads, from_left, from_right), weight,
        (((own, model), BF16),),
    )
    late, _ = hold((rows, start_grad))
    (result,) = call(
        functools.partial(result_kernel, slots), "result", (),
        (index, middle, late), weight, (((own, model), BF16),),
    )

    def ended(came, kernel):
        return hold((came, kernel))[0]

    ends, bit = [grad], 1
    while bit < tiles:
        came = ended(swapped(theirs, "tile", bit), ends.pop(0) if ends else dq)
        mine = added(mine, came)
        bit *= 2
        if bit < tiles:
            rows = mine.shape[0] // 2
            mine, theirs = mine[:rows], mine[rows:]
    came = [swapped(mine[by * shard : (by + 1) * shard], "dp", by) for by in apart]
    came = ended(came, result)
    total = mine[:shard].astype(F32)
    for part in came:
        total = total + part.astype(F32)
    if not square:
        total = lax.psum(total.astype(BF16), "seq").astype(F32)
    return (result.reshape(latents.shape), start_grad.reshape(latents.shape), total)


def solution(mesh):
    in_specs = (
        P("dp", "seq", "tile", None),
        P("dp", "seq", "tile", None),
        P("dp", None, None),
        P(("dp", "tile"), None),
        P(("dp", "tile"), None),
        P(("dp", "tile"), None),
        P(("dp", "tile"), None),
        P("tile", None),
        P(),
    )
    out_specs = (
        P("dp", "seq", "tile", None),
        P("dp", "seq", "tile", None),
        P(("dp", "tile"), None),
    )
    return jax.shard_map(local, mesh=mesh, in_specs=in_specs, out_specs=out_specs, check_vma=False)
```

```python
import functools

import jax
import jax.numpy as jnp
import numpy as np
from jax import lax
from jax.experimental import pallas as pl
from jax.experimental.pallas import tpu as pltpu
from jax.sharding import PartitionSpec as P

HEADS = 8
HEAD_DIM = 72
WIDTH = HEADS * HEAD_DIM
EPSILON = 1e-06
MASKED = -1e30
SCALE = HEAD_DIM ** (-0.5)
BF16 = jnp.bfloat16
F32 = jnp.float32
VMEM_LIMIT = 16 * 1024 * 1024
PACK_LIMIT = 63 * 1024 * 1024
SHORT = pl.CostEstimate(flops=1024, bytes_accessed=1024, transcendentals=0)


def mm(a, b):
    return jnp.dot(a, b, preferred_element_type=F32)


def mm_nt(a, b):
    return lax.dot_general(a, b, (((1,), (1,)), ((), ())), preferred_element_type=F32)


def mm_tn(a, b):
    return lax.dot_general(a, b, (((0,), (0,)), ((), ())), preferred_element_type=F32)


def head_masks(kind):
    lane = lax.broadcasted_iota(jnp.int32, (1, WIDTH), 1)
    inside = [(lane >= HEAD_DIM * h) & (lane < HEAD_DIM * (h + 1)) for h in range(HEADS)]
    return [jnp.where(hit, 1.0, 0.0).astype(kind) for hit in inside]


def spread(rows):
    return jnp.concatenate([rows * mask for mask in head_masks(rows.dtype)], axis=0)


def collect(big):
    n = big.shape[0] // HEADS
    masks = head_masks(F32)
    total = big[:n] * masks[0]
    for h in range(1, HEADS):
        total = total + big[h * n : (h + 1) * n] * masks[h]
    return total


def softmax_of(spread_q, keys, allowed):
    n, m = allowed.shape
    scores = (mm_nt(spread_q, keys) * SCALE).reshape(HEADS, n, m)
    scores = jnp.where((allowed > 0)[None], scores, MASKED)
    raised = jnp.exp(scores - jnp.max(scores, axis=-1, keepdims=True))
    probs = raised / jnp.sum(raised, axis=-1, keepdims=True)
    return probs.reshape(HEADS * n, m)


def attention_back(spread_q, keys, values, probs, grad):
    spread_g = spread(grad)
    dprob = mm_nt(spread_g, values)
    delta = jnp.sum(probs * dprob, axis=-1, keepdims=True)
    dscore = (probs * (dprob - delta) * SCALE).astype(BF16)
    dquery = collect(mm(dscore, keys))
    dkeys = mm_tn(dscore, spread_q)
    dvalues = mm_tn(probs.astype(BF16), spread_g)
    return dquery, dkeys, dvalues


def inverse_of(values):
    return lax.rsqrt(jnp.mean(values * values, axis=-1, keepdims=True) + EPSILON)


def norm_back(values, gain, grad):
    inverse = inverse_of(values)
    scaled = grad * gain
    cubed = inverse * inverse * inverse
    return inverse * scaled - values * cubed * jnp.mean(scaled * values, axis=-1, keepdims=True)


def expander(source, rows=WIDTH):
    row = lax.broadcasted_iota(jnp.int32, (rows, source.shape[1]), 0)
    return jnp.where(row == source, 1.0, 0.0).astype(BF16)


def ahead(rows, weight, start, stop, slots):
    total = None
    for (at, count), ref in zip(slots, weight):
        term = mm(rows[:, at : at + count], ref[:, start:stop])
        total = term if total is None else total + term
    return total


def behind(grad, weight, start, stop, select):
    turned = grad.astype(F32).T.astype(BF16)
    parts = [mm(ref[:, start:stop], turned).astype(BF16) for ref in weight]
    return mm(select[...], jnp.concatenate(parts, axis=0)).T


def space_allowed(place, pattern, span, tiles):
    own = 2 * span
    row = lax.broadcasted_iota(jnp.int32, (own, 4 * span), 0)
    column = lax.broadcasted_iota(jnp.int32, (own, 4 * span), 1)
    tile_at = place[0]
    allowed = jnp.zeros((own, 4 * span), jnp.int32)
    for b in range(2):
        for r in range(4):
            block = 2 * tile_at - 1 + r
            inside = (block >= 0) & (block < 2 * tiles)
            seen = inside if r == b + 1 else inside & (pattern[b, r] == 1)
            here = (row >= b * span) & (row < (b + 1) * span)
            here = here & (column >= r * span) & (column < (r + 1) * span)
            allowed = allowed + jnp.where(here, seen.astype(jnp.int32), 0)
    return allowed


def fetch(sources, buffers, semaphores):
    copies = [
        pltpu.make_async_copy(source, buffer, semaphores.at[number])
        for number, (source, buffer) in enumerate(zip(sources, buffers))
    ]
    for copy in copies:
        copy.start()
    for copy in copies:
        copy.wait()


def columns(model):
    wide = -(-3 * WIDTH // 128) * 128
    return 0, wide, 2 * wide, 2 * wide + model


def pack_kernel(
    space_hbm, time_hbm, space_out_hbm, time_out_hbm, packed, half_ref,
    space_qkv, time_qkv, space_out, time_out, ready,
):
    fetch(
        (space_hbm, time_hbm, space_out_hbm, time_out_hbm),
        (space_qkv, time_qkv, space_out, time_out), ready,
    )
    outs = jnp.concatenate([space_out[...].astype(F32), time_out[...].astype(F32)], axis=0)
    parts = [space_qkv[...].astype(F32), time_qkv[...].astype(F32), outs]
    packed[...] = jnp.concatenate(parts, axis=1).astype(BF16)
    lanes = half_ref.shape[1]
    first = lax.axis_index("seq") == 0

    @pl.when(first)
    def _():
        half_ref[...] = packed[:, :lanes]

    @pl.when(jnp.logical_not(first))
    def _():
        half_ref[...] = packed[:, lanes:]


def send_kernel(cut, piece, by_tile, by_seq, over_tile, over_seq):
    at, lanes = 0, cut[1]
    if piece is not None:
        at = piece.shape[1]
        over_tile[:, :at] = piece[...]
        over_seq[:, :at] = piece[...]
    over_tile[:, at:] = by_seq[:, : cut[0]]
    over_seq[:, at:] = by_tile[:, cut[0] : lanes]


def place_columns(out_ref, row, full):
    rows = slice(row, row + full.shape[0])
    space, time, out, stop = columns(full.shape[1] - 6 * WIDTH)
    pad = jnp.zeros((full.shape[0], time - space - 3 * WIDTH), BF16)
    out_ref[rows, space : space + 3 * WIDTH] = full[:, : 3 * WIDTH].astype(BF16)
    out_ref[rows, space + 3 * WIDTH : time] = pad
    out_ref[rows, time : time + 3 * WIDTH] = full[:, 3 * WIDTH : 6 * WIDTH].astype(BF16)
    out_ref[rows, time + 3 * WIDTH : out] = pad
    out_ref[rows, out:stop] = full[:, 6 * WIDTH :].astype(BF16)


def join_kernel(layout, place, *refs):
    *refs, out_ref = refs
    blocks, at = [], 0
    for ranges in layout:
        taken = refs[at : at + len(ranges)]
        parts = [ref[:, start:stop].astype(F32) for ref, (start, stop) in zip(taken, ranges)]
        blocks.append((parts[0], parts[1:]))
        at += len(ranges)

    def write(first):
        rows = []
        for mine, other in blocks:
            sides = [mine, *other] if first else [*other, mine]
            rows.append(jnp.concatenate(sides, axis=1) if other else mine)
        place_columns(out_ref, 0, jnp.concatenate(rows, axis=0))

    pl.when(place[1] == 0)(lambda: write(True))
    pl.when(place[1] != 0)(lambda: write(False))


def order_kernel(index_ref, order_ref):
    order_ref[...] = expander(index_ref[0:1, :], order_ref.shape[0])


def normed_kernel(order_ref, before, x_ref, after, mod_ref, normed_ref):
    x = jnp.concatenate([before[...], x_ref[...], after[...]], axis=0).astype(F32)
    normed = (x * inverse_of(x) * (1.0 + mod_ref[0:1, :])).astype(BF16)
    normed_ref[...] = mm(normed, order_ref[...]).astype(BF16)


def early_kernel(slots, normed_ref, weight, partial_ref):
    partial_ref[...] = ahead(normed_ref, weight, 0, 3 * WIDTH, slots)


def forward_kernel(tiles, slots, late, place, pattern, normed_ref, *refs):
    *partial, weight, q_ref, kv_ref, att_ref, probs_ref = refs
    own = q_ref.shape[0]
    span = own // 2
    rows = ahead(
        normed_ref, [weight[n] for n in late], 0, 3 * WIDTH, [slots[n] for n in late]
    )
    for earlier in partial:
        rows = rows + earlier[...]
    rows = rows.astype(BF16)
    query, kv = rows[span : span + own, :WIDTH], rows[:, WIDTH:]
    keys, values = kv[:, :WIDTH], kv[:, WIDTH:]
    q_ref[...] = query
    kv_ref[...] = kv
    allowed = space_allowed(place, pattern, span, tiles)
    probs = softmax_of(spread(query), keys, allowed)
    probs_ref[...] = probs
    att_ref[...] = collect(mm(probs.astype(BF16), values)).astype(BF16)


def middle_of(slots, index_ref, order_ref, x_ref, mod_ref, att, weight):
    _, time, out, stop = columns(x_ref.shape[1])
    att = mm(att, expander(index_ref[1:2, :])).astype(BF16)
    middle = x_ref[...].astype(F32) + ahead(att, weight, out, stop, slots)
    normed = (middle * inverse_of(middle) * (1.0 + mod_ref[1:2, :])).astype(BF16)
    normed = mm(normed, order_ref[...]).astype(BF16)
    return middle, ahead(normed, weight, time, time + 3 * WIDTH, slots).astype(BF16)


def middle_kernel(slots, index_ref, order_ref, x_ref, mod_ref, att_ref, weight, middle_ref, rows_ref):
    middle, rows = middle_of(slots, index_ref, order_ref, x_ref, mod_ref, att_ref[...], weight)
    middle_ref[...] = middle
    rows_ref[...] = rows


def att_grad_kernel(parts, row, index_ref, *refs):
    upstream = jnp.concatenate([ref[...] for ref in refs[:parts]], axis=0).astype(BF16)
    weight, grad_ref = refs[parts:]
    *_, out, stop = columns(upstream.shape[1])
    select = expander(index_ref[row : row + 1, :])
    grad_ref[...] = behind(upstream, weight, out, stop, select).astype(BF16)


def time_att_kernel(allowed_ref, rows_ref, grad_ref, out_ref):
    rows = rows_ref[...]
    query, keys, values = rows[:, :WIDTH], rows[:, WIDTH : 2 * WIDTH], rows[:, 2 * WIDTH :]
    spread_q = spread(query)
    probs = softmax_of(spread_q, keys, allowed_ref[...])
    att = collect(mm(probs.astype(BF16), values))
    grads = attention_back(spread_q, keys, values, probs, grad_ref[...])
    out_ref[...] = jnp.concatenate(grads + (att,), axis=1).astype(BF16)


def time_pair_kernel(
    slots, place, time_mask, index_ref, order_ref, mod_ref, x_ref, space_ref, own_ref, grad_ref,
    weight, out_ref, att_ref,
):
    count = own_ref.shape[0]
    first = place[1] == 0

    def frames(own, other):
        own, other = own.astype(F32), other.astype(F32)
        return jnp.where(first, own, other), jnp.where(first, other, own)

    _, other = middle_of(slots, index_ref, order_ref, x_ref, mod_ref, space_ref[...], weight)
    own = own_ref[...]
    row = lax.broadcasted_iota(jnp.int32, (WIDTH, 128), 0)
    low = lax.broadcasted_iota(jnp.int32, (WIDTH, 128), 1) * HEAD_DIM
    heads = jnp.where((row >= low) & (row < low + HEAD_DIM), 1.0, 0.0).astype(BF16)

    def summed(product):
        high = product.astype(BF16)
        return mm(high, heads) + mm((product - high.astype(F32)).astype(BF16), heads)

    def widened(value):
        return mm_nt(value.astype(BF16), heads)

    _, q1 = frames(own[:, :WIDTH], other[:, :WIDTH])
    k0, k1 = frames(own[:, WIDTH : 2 * WIDTH], other[:, WIDTH : 2 * WIDTH])
    v0, v1 = frames(own[:, 2 * WIDTH :], other[:, 2 * WIDTH :])
    g0, g1 = frames(grad_ref[:count, :], grad_ref[count:, :])
    s10 = jnp.where(time_mask[1, 0] == 1, summed(q1 * k0) * SCALE, MASKED)
    s11 = summed(q1 * k1) * SCALE
    top = jnp.maximum(s10, s11)
    e10, e11 = jnp.exp(s10 - top), jnp.exp(s11 - top)
    total = e10 + e11
    p10, p11 = e10 / total, e11 / total
    dp10, dp11 = summed(g1 * v0), summed(g1 * v1)
    delta = p10 * dp10 + p11 * dp11
    d10, d11 = widened(p10 * (dp10 - delta) * SCALE), widened(p11 * (dp11 - delta) * SCALE)
    w10, w11 = widened(p10), widened(p11)
    att1 = w10 * v0 + w11 * v1
    zero = jnp.zeros_like(q1)
    of_frame0 = (zero, d10 * q1, g0 + w10 * g1, v0)
    of_frame1 = (d10 * k0 + d11 * k1, d11 * q1, w11 * g1, att1)
    mine = [jnp.where(first, a, b) for a, b in zip(of_frame0, of_frame1)]
    out_ref[...] = jnp.concatenate(mine, axis=1).astype(BF16)
    theirs = jnp.where(first, att1, v0)
    att_ref[...] = jnp.concatenate([mine[3], theirs], axis=0).astype(BF16)


def term_kernel(parts, index_ref, att_ref, *refs):
    ups, (mine_ref, theirs_ref) = refs[:parts], refs[parts:]
    att = mm(att_ref[...], expander(index_ref[...])).astype(BF16)
    count = ups[0].shape[0]
    term = mm_tn(att[:count], ups[0][...])
    if parts > 1:
        other = jnp.concatenate([ref[...] for ref in ups[1:]], axis=0)
        term = term + mm_tn(att[count:], other)
    half = mine_ref.shape[0]
    term = term.astype(BF16)
    mine_ref[...] = term[:half]
    theirs_ref[...] = term[half:]


def middle_back_kernel(
    order_ref, up_ref, mod_ref, middle_ref, rows_ref, weight, grad_ref
):
    middle = middle_ref[...]
    _, time, *_ = columns(middle.shape[1])
    back = behind(rows_ref[:, : 3 * WIDTH], weight, time, time + 3 * WIDTH, order_ref)
    gain = 1.0 + mod_ref[1:2, :]
    grad = up_ref[...].astype(F32) + norm_back(middle, gain, back)
    grad_ref[...] = grad


def result_kernel(slots, index_ref, middle_ref, rows_ref, weight, result_ref):
    att = mm(rows_ref[:, 3 * WIDTH :], expander(index_ref[2:3, :])).astype(BF16)
    *_, out, stop = columns(middle_ref.shape[1])
    grown = ahead(att, weight, out, stop, slots)
    result_ref[...] = (middle_ref[...] + grown).astype(BF16)


def space_back_kernel(
    q_ref, kv_ref, probs_ref, att_grad_ref, dq_ref, own_ref, low_ref, high_ref
):
    span = low_ref.shape[0]
    keys, values = kv_ref[:, :WIDTH], kv_ref[:, WIDTH:]
    dquery, dkeys, dvalues = attention_back(
        spread(q_ref[...]), keys, values, probs_ref[...], att_grad_ref[...]
    )
    dq_ref[...] = dquery.astype(BF16)
    both = jnp.concatenate([dkeys, dvalues], axis=1)
    low_ref[...] = both[:span].astype(BF16)
    own_ref[...] = both[span : 3 * span]
    high_ref[...] = both[3 * span :].astype(BF16)


def start_back_kernel(
    order_ref, x_ref, mod_ref, grad_ref, dq_ref, own_ref, left, right, weight, out_ref
):
    x = x_ref[...].astype(F32)
    rim = jnp.concatenate([left[...], right[...]], axis=0).astype(F32)
    dkv = own_ref[...] + rim
    grads = jnp.concatenate([dq_ref[...].astype(F32), dkv], axis=1).astype(BF16)
    back = behind(grads, weight, 0, 3 * WIDTH, order_ref)
    gain = 1.0 + mod_ref[0:1, :]
    out_ref[...] = (grad_ref[...] + norm_back(x, gain, back)).astype(BF16)


VMEM = pl.BlockSpec(memory_space=pltpu.VMEM)
SMEM = pl.BlockSpec(memory_space=pltpu.SMEM)


HBM = pl.BlockSpec(memory_space=pltpu.HBM)


def call(kernel, name, scalars, arrays, weight, outs, scratch=(), far=(), grant=VMEM_LIMIT, cost=None):
    plain = len(scalars) + len(arrays) + len(far)
    weight, tree = jax.tree.flatten(list(weight))

    def body(*refs):
        fixed, pieces = refs[:plain], refs[plain : plain + len(weight)]
        pieces = (jax.tree.unflatten(tree, pieces),) if pieces else ()
        kernel(*fixed, *pieces, *refs[plain + len(weight) :])

    outs = [jax.ShapeDtypeStruct(shape, kind) for shape, kind in outs]
    near = [pltpu.VMEM(array.shape, array.dtype) for array in far]
    if far:
        near.append(pltpu.SemaphoreType.DMA((len(far),)))
    specs = [SMEM] * len(scalars) + [VMEM] * len(arrays) + [HBM] * len(far) + [VMEM] * len(weight)
    return pl.pallas_call(
        body,
        name=name,
        in_specs=specs,
        out_specs=[VMEM] * len(outs),
        out_shape=outs,
        scratch_shapes=near + list(scratch),
        compiler_params=pltpu.CompilerParams(vmem_limit_bytes=grant),
        cost_estimate=cost,
    )(*scalars, *arrays, *far, *weight)


def swapped(array, axis, bit):
    count = lax.axis_size(axis)
    return lax.ppermute(array, axis, [(i, i ^ bit) for i in range(count)])


def added(a, b):
    return (a.astype(F32) + b.astype(F32)).astype(BF16)


def relative_rows(shard, tile_at, clip_at, tiles, clips):
    block, inner = np.arange(clips * tiles * shard) // shard, np.arange(clips * tiles * shard) % shard
    low, apart, high = block // (2 * clips), block // 2 % clips, block % 2
    tile, clip = tile_at ^ (low + 2 * high), (clip_at + clips - apart) % clips
    return (clip * tiles + tile) * shard + inner


def local(
    latents,
    upstream,
    modulation,
    space_qkv,
    space_out,
    time_qkv,
    time_out,
    space_pattern,
    time_mask,
):
    seq, tiles, clips = lax.axis_size("seq"), lax.axis_size("tile"), lax.axis_size("dp")
    own, model = latents.shape[2], latents.shape[3]
    span, half = own // 2, own // 2
    shard = space_out.shape[0]
    x = latents.reshape(own, model)
    up = upstream.reshape(own, model)
    mod = modulation.reshape(modulation.shape[1:])
    tile_at, seq_at, clip_at = lax.axis_index("tile"), lax.axis_index("seq"), lax.axis_index("dp")
    side = seq_at if seq == 2 else jnp.zeros((), jnp.int32)
    place = jnp.stack([tile_at, side]).astype(jnp.int32)

    square = seq == 2 and tiles == 4
    hold = lax.optimization_barrier
    width = 6 * WIDTH + model
    own_w, half_w = call(
        pack_kernel, "pack", (), (), (),
        (((2 * shard, width), BF16), ((2 * shard, width // 2), BF16)),
        far=(space_qkv, time_qkv, space_out, time_out), grant=PACK_LIMIT,
    )
    if square:
        order = relative_rows(2 * shard, tile_at, clip_at, tiles, clips)
    else:
        order = jnp.arange(model)

    inner = order // (2 * shard) * shard + order % shard
    later = order % (2 * shard) >= shard
    space_rows = jnp.where((order >= 0) & ~later, inner, -1)
    time_rows = jnp.where((order >= 0) & later, inner, -1)
    index = jnp.stack([order, space_rows, time_rows]).astype(jnp.int32)
    near = np.arange(WIDTH) // shard
    bits = tiles.bit_length() - 1
    first = near // clips
    rel_tile = sum(((first >> b) & 1) << (bits - 1 - b) for b in range(bits))
    owner = (clip_at ^ (near % clips)) * tiles + (tile_at ^ rel_tile)
    terms = (owner * shard + np.arange(WIDTH) % shard).astype(jnp.int32).reshape(1, WIDTH)

    rise = [(i, i + 1) for i in range(tiles - 1)]
    fall = [(i + 1, i) for i in range(tiles - 1)]

    def rims(rows):
        before = lax.ppermute(rows[span:], "tile", rise)
        return before, lax.ppermute(rows[:span], "tile", fall)

    def joined(blocks):
        layout = [[(start, stop) for _, start, stop in block] for block in blocks]
        arrays = [array for block in blocks for array, _, _ in block]
        shape = (len(blocks) * 2 * shard, columns(model)[-1])
        return functools.partial(join_kernel, layout), arrays, (shape, BF16)

    def whole(array):
        return (array, 0, array.shape[1])

    (made,) = call(order_kernel, "order", (), (index,), (), (((model, model), BF16),))

    def normed_of(order, before, rows, after):
        return call(
            normed_kernel, "normed", (), (order, before, rows, after, mod), (),
            (((2 * own, model), BF16),),
        )[0]

    if square:
        lanes = width // 2
        cut = lanes // 256 * 128

        def onward(piece):
            return lax.ppermute(piece, "dp", [(i, (i + 1) % clips) for i in range(clips)])

        def near_rows(piece, sides):
            return [(piece, 0, lanes), (sides[1], 0, lanes)]

        def far_rows(sides, later):
            low, high = (part.shape[1] for part in later)
            return [
                (sides[0], 0, lanes),
                (later[0], low - cut, low), (later[1], high - (lanes - cut), high),
            ]

        def sends(piece, by_tile, by_seq, blocks=()):
            arrays = [by_tile, by_seq] if piece is None else [piece, by_tile, by_seq]
            at, count = (0 if piece is None else lanes), len(arrays)
            join, parts, shape = joined(blocks)

            def kernel(place_ref, *refs):
                sides, earlier = refs[:count], refs[count : count + len(parts)]
                outs = refs[count + len(parts) :]
                sides = sides if piece is not None else (None,) + sides
                send_kernel((cut, lanes), *sides, *outs[:2])
                if parts:
                    join(place_ref, *earlier, outs[2])

            outs = [((2 * shard, at + cut), BF16), ((2 * shard, at + lanes - cut), BF16)]
            if parts:
                outs.append(shape)
            over_tile, over_seq, *group = call(
                kernel, "send", (place,), (*arrays, *parts), (), outs
            )
            return group, (swapped(over_tile, "tile", 2), swapped(over_seq, "seq", 1))

        across = swapped(own_w, "tile", 2)
        piece, other_x, early = hold((onward(half_w), swapped(x, "seq", 1), x))
        pieces, came, groups, others = [piece], [], [], []
        for step in range(clips):
            piece = pieces[step] if step < clips - 1 else None
            following = onward(piece) if step < clips - 2 else ()
            if step == 0:
                moves = swapped(piece, "tile", 2), swapped(piece, "seq", 1)
                later_up, _ = hold((up, piece))
                moves, across, other_up = hold((moves, across, swapped(later_up[:half], "seq", 1)))
            else:
                blocks = [[whole(own_w)], [whole(across)]] if step == 2 else []
                if step > 1:
                    blocks.append(near_rows(pieces[step - 2], came[step - 2]))
                    blocks.append(far_rows(came[step - 2], came[step - 1]))
                if step == clips - 1:
                    blocks.append(near_rows(pieces[step - 1], came[step - 1]))
                group, moves = sends(piece, *came[-1], blocks)
                if group:
                    groups += group
                    others.append(swapped(groups[-1], "tile", 1))
            if step == 1:
                moves, made = hold((moves, made))
            if step == clips - 2:
                early, *_ = hold((early, came[-1]))
                moves, before, after = hold((moves, *rims(early)))
            if step == clips - 1:
                normed = normed_of(made, before, x, after)
                at = groups[0].shape[0]
                (partial,) = call(
                    functools.partial(early_kernel, [(0, at), (at, groups[1].shape[0]), (model // 2, at)]),
                    "space_early", (), (normed,), [*groups[:2], others[0]],
                    (((2 * own, 3 * WIDTH), F32),), cost=SHORT,
                )
                late = normed
                moves, normed, partial = hold((moves, normed, partial))
            moves, following, others = hold((moves, following, others))
            came.append(moves)
            if step < clips - 2:
                pieces.append(following)
        order = made
        late_up, _ = hold((up, late))
        other_up = other_up, swapped(late_up[half:], "seq", 1)
        join, parts, shape = joined([far_rows(came[-2], came[-1])])
        groups += call(join, "join", (place,), parts, (), (shape,))
        others.append(swapped(groups[-1], "tile", 1))
        weight = groups + others
        late, partial = [2, 4, 5], (partial,)
    else:
        before, after = rims(x)
        order = made
        normed = normed_of(order, before, x, after)
        join, parts, shape = joined([[whole(own_w)]])
        (laid,) = call(join, "join", (place,), parts, (), (shape,))
        weight = [lax.all_gather(laid, ("dp", "tile"), axis=0, tiled=True)]
        late, partial = [0], ()
    ends = np.cumsum([0] + [part.shape[0] for part in weight]).tolist()
    slots = [(at, part.shape[0]) for at, part in zip(ends, weight)]

    query, window, att, probs = call(
        functools.partial(forward_kernel, tiles, slots, late), "forward", (place, space_pattern),
        (normed,) + partial, weight,
        (
            ((own, WIDTH), BF16), ((2 * own, 2 * WIDTH), BF16), ((own, WIDTH), BF16),
            ((HEADS * own, 2 * own), F32),
        ),
        cost=SHORT,
    )
    middle, rows = call(
        functools.partial(middle_kernel, slots), "middle", (), (index, order, x, mod, att), weight,
        (((own, model), F32), ((own, 3 * WIDTH), BF16)), cost=SHORT,
    )
    if square:
        ups = (up,) + other_up
        other_att = swapped(att, "seq", 1)
    else:
        def turned(array):
            parts = array.reshape(seq, own // seq, array.shape[1])
            parts = lax.all_to_all(parts, "seq", split_axis=0, concat_axis=0, tiled=True)
            return parts.reshape(array.shape)

        ups = (turned(up),)
    (time_att_grad,) = call(
        functools.partial(att_grad_kernel, len(ups), 2), "att_grad", (), (index,) + ups, weight,
        ((((2 if square else 1) * own, WIDTH), BF16),),
    )
    if square:
        rows, att = call(
            functools.partial(time_pair_kernel, slots), "time_att", (place, time_mask),
            (index, order, mod, other_x, other_att, rows, time_att_grad), weight,
            (((own, 4 * WIDTH), BF16), ((2 * own, WIDTH), BF16)),
        )
    else:
        token = jnp.arange(own)
        frame, patch = token // (own // seq), token % (own // seq)
        seen = jnp.take(jnp.take(time_mask, frame, axis=0), frame, axis=1) == 1
        seen = (seen & (frame[None, :] < frame[:, None])) | (frame[None, :] == frame[:, None])
        allowed = (seen & (patch[None, :] == patch[:, None])).astype(jnp.int32)
        (rows,) = call(
            time_att_kernel, "time_att", (), (allowed, turned(rows), time_att_grad), (),
            (((own, 4 * WIDTH), BF16),),
        )
        att = rows[:, 3 * WIDTH :]
        rows = turned(rows)
    mine, theirs = call(
        functools.partial(term_kernel, len(ups)), "term", (), (terms, att) + ups, (),
        (((WIDTH // 2, model), BF16),) * 2,
    )

    (grad,) = call(
        middle_back_kernel, "middle_back", (), (order, up, mod, middle, rows), weight,
        (((own, model), F32),),
    )
    (att_grad,) = call(
        functools.partial(att_grad_kernel, 1, 1), "space_grad", (), (index, grad), weight,
        (((own, WIDTH), BF16),),
    )
    dq, own_grads, to_left, to_right = call(
        space_back_kernel, "space_back", (), (query, window, probs, att_grad), (),
        (
            ((own, WIDTH), BF16), ((own, 2 * WIDTH), F32),
            ((span, 2 * WIDTH), BF16), ((span, 2 * WIDTH), BF16),
        ),
    )
    from_left = lax.ppermute(to_right, "tile", rise)
    from_right = lax.ppermute(to_left, "tile", fall)
    (start_grad,) = call(
        start_back_kernel, "start_back", (),
        (order, x, mod, grad, dq, own_grads, from_left, from_right), weight,
        (((own, model), BF16),),
    )
    late, _ = hold((rows, start_grad))
    (result,) = call(
        functools.partial(result_kernel, slots), "result", (),
        (index, middle, late), weight, (((own, model), BF16),),
    )

    def ended(came, kernel):
        return hold((came, kernel))[0]

    ends, bit = [grad], 1
    while bit < tiles:
        came = ended(swapped(theirs, "tile", bit), ends.pop(0) if ends else dq)
        mine = added(mine, came)
        bit *= 2
        if bit < tiles:
            rows = mine.shape[0] // 2
            mine, theirs = mine[:rows], mine[rows:]
    came = [swapped(mine[by * shard : (by + 1) * shard], "dp", by) for by in range(1, clips)]
    came = [ended(came[0], result)] + ended(came[1:], start_grad)
    total = mine[:shard].astype(F32)
    for part in came:
        total = total + part.astype(F32)
    if not square:
        total = lax.psum(total.astype(BF16), "seq").astype(F32)
    return (result.reshape(latents.shape), start_grad.reshape(latents.shape), total)


def solution(mesh):
    in_specs = (
        P("dp", "seq", "tile", None),
        P("dp", "seq", "tile", None),
        P("dp", None, None),
        P(("dp", "tile"), None),
        P(("dp", "tile"), None),
        P(("dp", "tile"), None),
        P(("dp", "tile"), None),
        P("tile", None),
        P(),
    )
    out_specs = (
        P("dp", "seq", "tile", None),
        P("dp", "seq", "tile", None),
        P(("dp", "tile"), None),
    )
    return jax.shard_map(local, mesh=mesh, in_specs=in_specs, out_specs=out_specs, check_vma=False)
```

```python
import functools

import jax
import jax.numpy as jnp
import numpy as np
from jax import lax
from jax.experimental import pallas as pl
from jax.experimental.pallas import tpu as pltpu
from jax.sharding import PartitionSpec as P

HEADS = 8
HEAD_DIM = 72
WIDTH = HEADS * HEAD_DIM
EPSILON = 1e-06
MASKED = -1e30
SCALE = HEAD_DIM ** (-0.5)
BF16 = jnp.bfloat16
F32 = jnp.float32
VMEM_LIMIT = 16 * 1024 * 1024
PACK_LIMIT = 63 * 1024 * 1024
SHORT = pl.CostEstimate(flops=1024, bytes_accessed=1024, transcendentals=0)


def mm(a, b):
    return jnp.dot(a, b, preferred_element_type=F32)


def mm_nt(a, b):
    return lax.dot_general(a, b, (((1,), (1,)), ((), ())), preferred_element_type=F32)


def mm_tn(a, b):
    return lax.dot_general(a, b, (((0,), (0,)), ((), ())), preferred_element_type=F32)


def head_masks(kind):
    lane = lax.broadcasted_iota(jnp.int32, (1, WIDTH), 1)
    inside = [(lane >= HEAD_DIM * h) & (lane < HEAD_DIM * (h + 1)) for h in range(HEADS)]
    return [jnp.where(hit, 1.0, 0.0).astype(kind) for hit in inside]


def spread(rows):
    return jnp.concatenate([rows * mask for mask in head_masks(rows.dtype)], axis=0)


def collect(big):
    n = big.shape[0] // HEADS
    masks = head_masks(F32)
    total = big[:n] * masks[0]
    for h in range(1, HEADS):
        total = total + big[h * n : (h + 1) * n] * masks[h]
    return total


def softmax_of(spread_q, keys, allowed):
    n, m = allowed.shape
    scores = (mm_nt(spread_q, keys) * SCALE).reshape(HEADS, n, m)
    scores = jnp.where((allowed > 0)[None], scores, MASKED)
    raised = jnp.exp(scores - jnp.max(scores, axis=-1, keepdims=True))
    probs = raised / jnp.sum(raised, axis=-1, keepdims=True)
    return probs.reshape(HEADS * n, m)


def attention_back(spread_q, keys, values, probs, grad):
    spread_g = spread(grad)
    dprob = mm_nt(spread_g, values)
    delta = jnp.sum(probs * dprob, axis=-1, keepdims=True)
    dscore = (probs * (dprob - delta) * SCALE).astype(BF16)
    dquery = collect(mm(dscore, keys))
    dkeys = mm_tn(dscore, spread_q)
    dvalues = mm_tn(probs.astype(BF16), spread_g)
    return dquery, dkeys, dvalues


def inverse_of(values):
    return lax.rsqrt(jnp.mean(values * values, axis=-1, keepdims=True) + EPSILON)


def norm_back(values, gain, grad):
    inverse = inverse_of(values)
    scaled = grad * gain
    cubed = inverse * inverse * inverse
    return inverse * scaled - values * cubed * jnp.mean(scaled * values, axis=-1, keepdims=True)


def expander(source, rows=WIDTH):
    row = lax.broadcasted_iota(jnp.int32, (rows, source.shape[1]), 0)
    return jnp.where(row == source, 1.0, 0.0).astype(BF16)


def ahead(rows, weight, start, stop, slots):
    total = None
    for (at, count), ref in zip(slots, weight):
        term = mm(rows[:, at : at + count], ref[:, start:stop])
        total = term if total is None else total + term
    return total


def behind(grad, weight, start, stop, select, rounded=False):
    count = grad.shape[0]
    turned = grad.astype(F32).T.astype(BF16)
    parts = [mm(ref[:, start:stop], turned) for ref in weight]
    part = jnp.concatenate(parts, axis=0)
    high = part.astype(BF16)
    if rounded:
        return mm(select[...], high).T.astype(BF16)
    low = (part - high.astype(F32)).astype(BF16)
    both = mm(select[...], jnp.concatenate([high, low], axis=1))
    return (both[:, :count] + both[:, count:]).T


def space_allowed(place, pattern, span, tiles):
    own = 2 * span
    row = lax.broadcasted_iota(jnp.int32, (own, 4 * span), 0)
    column = lax.broadcasted_iota(jnp.int32, (own, 4 * span), 1)
    tile_at = place[0]
    allowed = jnp.zeros((own, 4 * span), jnp.int32)
    for b in range(2):
        for r in range(4):
            block = 2 * tile_at - 1 + r
            inside = (block >= 0) & (block < 2 * tiles)
            seen = inside if r == b + 1 else inside & (pattern[b, r] == 1)
            here = (row >= b * span) & (row < (b + 1) * span)
            here = here & (column >= r * span) & (column < (r + 1) * span)
            allowed = allowed + jnp.where(here, seen.astype(jnp.int32), 0)
    return allowed


def fetch(sources, buffers, semaphores):
    copies = [
        pltpu.make_async_copy(source, buffer, semaphores.at[number])
        for number, (source, buffer) in enumerate(zip(sources, buffers))
    ]
    for copy in copies:
        copy.start()
    for copy in copies:
        copy.wait()


def columns(model):
    wide = -(-3 * WIDTH // 128) * 128
    return 0, wide, 2 * wide, 2 * wide + model


def pack_kernel(
    space_hbm, time_hbm, space_out_hbm, time_out_hbm, packed, half_ref,
    space_qkv, time_qkv, space_out, time_out, ready,
):
    fetch(
        (space_hbm, time_hbm, space_out_hbm, time_out_hbm),
        (space_qkv, time_qkv, space_out, time_out), ready,
    )
    outs = jnp.concatenate([space_out[...].astype(F32), time_out[...].astype(F32)], axis=0)
    packed[:, : 3 * WIDTH] = space_qkv[...]
    packed[:, 3 * WIDTH : 6 * WIDTH] = time_qkv[...]
    packed[:, 6 * WIDTH :] = outs.astype(BF16)
    lanes = half_ref.shape[1]
    first = lax.axis_index("seq") == 0

    @pl.when(first)
    def _():
        half_ref[...] = packed[:, :lanes]

    @pl.when(jnp.logical_not(first))
    def _():
        half_ref[...] = packed[:, lanes:]


def send_kernel(cut, piece, by_tile, by_seq, over_tile, over_seq):
    at, lanes = 0, cut[1]
    if piece is not None:
        at = piece.shape[1]
        over_tile[:, :at] = piece[...]
        over_seq[:, :at] = piece[...]
    over_tile[:, at:] = by_seq[:, : cut[0]]
    over_seq[:, at:] = by_tile[:, cut[0] : lanes]


def place_columns(out_ref, row, full):
    rows = slice(row, row + full.shape[0])
    space, time, out, stop = columns(full.shape[1] - 6 * WIDTH)
    pad = jnp.zeros((full.shape[0], time - space - 3 * WIDTH), BF16)
    out_ref[rows, space : space + 3 * WIDTH] = full[:, : 3 * WIDTH].astype(BF16)
    out_ref[rows, space + 3 * WIDTH : time] = pad
    out_ref[rows, time : time + 3 * WIDTH] = full[:, 3 * WIDTH : 6 * WIDTH].astype(BF16)
    out_ref[rows, time + 3 * WIDTH : out] = pad
    out_ref[rows, out:stop] = full[:, 6 * WIDTH :].astype(BF16)


def join_kernel(layout, place, *refs):
    *refs, out_ref = refs
    blocks, at = [], 0
    for ranges in layout:
        taken = refs[at : at + len(ranges)]
        parts = [ref[:, start:stop].astype(F32) for ref, (start, stop) in zip(taken, ranges)]
        blocks.append((parts[0], parts[1:]))
        at += len(ranges)

    def write(first):
        rows = []
        for mine, other in blocks:
            sides = [mine, *other] if first else [*other, mine]
            rows.append(jnp.concatenate(sides, axis=1) if other else mine)
        place_columns(out_ref, 0, jnp.concatenate(rows, axis=0))

    pl.when(place[1] == 0)(lambda: write(True))
    pl.when(place[1] != 0)(lambda: write(False))


def order_kernel(index_ref, order_ref):
    order_ref[...] = expander(index_ref[0:1, :], order_ref.shape[0])


def normed_kernel(order_ref, before, x_ref, after, mod_ref, normed_ref):
    x = jnp.concatenate([before[...], x_ref[...], after[...]], axis=0).astype(F32)
    normed = (x * inverse_of(x) * (1.0 + mod_ref[0:1, :])).astype(BF16)
    normed_ref[...] = mm(normed, order_ref[...]).astype(BF16)


def early_kernel(slots, normed_ref, weight, partial_ref):
    partial_ref[...] = ahead(normed_ref, weight, 0, 3 * WIDTH, slots)


def forward_kernel(tiles, slots, late, place, pattern, normed_ref, *refs):
    *partial, weight, q_ref, kv_ref, att_ref, probs_ref = refs
    own = q_ref.shape[0]
    span = own // 2
    rows = ahead(
        normed_ref, [weight[n] for n in late], 0, 3 * WIDTH, [slots[n] for n in late]
    )
    for earlier in partial:
        rows = rows + earlier[...]
    rows = rows.astype(BF16)
    query, kv = rows[span : span + own, :WIDTH], rows[:, WIDTH:]
    keys, values = kv[:, :WIDTH], kv[:, WIDTH:]
    q_ref[...] = query
    kv_ref[...] = kv
    allowed = space_allowed(place, pattern, span, tiles)
    probs = softmax_of(spread(query), keys, allowed)
    probs_ref[...] = probs
    att_ref[...] = collect(mm(probs.astype(BF16), values)).astype(BF16)


def middle_of(slots, index_ref, order_ref, x_ref, mod_ref, att, weight):
    _, time, out, stop = columns(x_ref.shape[1])
    att = mm(att, expander(index_ref[1:2, :])).astype(BF16)
    middle = x_ref[...].astype(F32) + ahead(att, weight, out, stop, slots)
    normed = (middle * inverse_of(middle) * (1.0 + mod_ref[1:2, :])).astype(BF16)
    normed = mm(normed, order_ref[...]).astype(BF16)
    return middle, ahead(normed, weight, time, time + 3 * WIDTH, slots).astype(BF16)


def middle_kernel(slots, index_ref, order_ref, x_ref, mod_ref, att_ref, weight, middle_ref, rows_ref):
    middle, rows = middle_of(slots, index_ref, order_ref, x_ref, mod_ref, att_ref[...], weight)
    middle_ref[...] = middle
    rows_ref[...] = rows


def att_grad_kernel(parts, row, index_ref, *refs):
    upstream = jnp.concatenate([ref[...] for ref in refs[:parts]], axis=0).astype(BF16)
    weight, grad_ref = refs[parts:]
    *_, out, stop = columns(upstream.shape[1])
    grad_ref[...] = behind(
        upstream, weight, out, stop, expander(index_ref[row : row + 1, :]), rounded=True
    )


def time_att_kernel(allowed_ref, rows_ref, grad_ref, out_ref):
    rows = rows_ref[...]
    query, keys, values = rows[:, :WIDTH], rows[:, WIDTH : 2 * WIDTH], rows[:, 2 * WIDTH :]
    spread_q = spread(query)
    probs = softmax_of(spread_q, keys, allowed_ref[...])
    att = collect(mm(probs.astype(BF16), values))
    grads = attention_back(spread_q, keys, values, probs, grad_ref[...])
    out_ref[...] = jnp.concatenate(grads + (att,), axis=1).astype(BF16)


def time_pair_kernel(
    slots, place, time_mask, index_ref, order_ref, mod_ref, x_ref, space_ref, own_ref, grad_ref,
    weight, out_ref, att_ref,
):
    count = own_ref.shape[0]
    first = place[1] == 0

    def frames(own, other):
        own, other = own.astype(F32), other.astype(F32)
        return jnp.where(first, own, other), jnp.where(first, other, own)

    _, other = middle_of(slots, index_ref, order_ref, x_ref, mod_ref, space_ref[...], weight)
    own = own_ref[...]
    row = lax.broadcasted_iota(jnp.int32, (WIDTH, 128), 0)
    low = lax.broadcasted_iota(jnp.int32, (WIDTH, 128), 1) * HEAD_DIM
    heads = jnp.where((row >= low) & (row < low + HEAD_DIM), 1.0, 0.0).astype(BF16)

    def summed(product):
        high = product.astype(BF16)
        return mm(high, heads) + mm((product - high.astype(F32)).astype(BF16), heads)

    def widened(value):
        return mm_nt(value.astype(BF16), heads)

    _, q1 = frames(own[:, :WIDTH], other[:, :WIDTH])
    k0, k1 = frames(own[:, WIDTH : 2 * WIDTH], other[:, WIDTH : 2 * WIDTH])
    v0, v1 = frames(own[:, 2 * WIDTH :], other[:, 2 * WIDTH :])
    g0, g1 = frames(grad_ref[:count, :], grad_ref[count:, :])
    s10 = jnp.where(time_mask[1, 0] == 1, summed(q1 * k0) * SCALE, MASKED)
    s11 = summed(q1 * k1) * SCALE
    top = jnp.maximum(s10, s11)
    e10, e11 = jnp.exp(s10 - top), jnp.exp(s11 - top)
    total = e10 + e11
    p10, p11 = e10 / total, e11 / total
    dp10, dp11 = summed(g1 * v0), summed(g1 * v1)
    delta = p10 * dp10 + p11 * dp11
    d10, d11 = widened(p10 * (dp10 - delta) * SCALE), widened(p11 * (dp11 - delta) * SCALE)
    w10, w11 = widened(p10), widened(p11)
    att1 = w10 * v0 + w11 * v1
    zero = jnp.zeros_like(q1)
    of_frame0 = (zero, d10 * q1, g0 + w10 * g1, v0)
    of_frame1 = (d10 * k0 + d11 * k1, d11 * q1, w11 * g1, att1)
    mine = [jnp.where(first, a, b) for a, b in zip(of_frame0, of_frame1)]
    out_ref[...] = jnp.concatenate(mine, axis=1).astype(BF16)
    theirs = jnp.where(first, att1, v0)
    att_ref[...] = jnp.concatenate([mine[3], theirs], axis=0).astype(BF16)


def term_kernel(parts, index_ref, att_ref, *refs):
    ups, (mine_ref, theirs_ref) = refs[:parts], refs[parts:]
    att = mm(att_ref[...], expander(index_ref[...])).astype(BF16)
    count = ups[0].shape[0]
    term = mm_tn(att[:count], ups[0][...])
    if parts > 1:
        other = jnp.concatenate([ref[...] for ref in ups[1:]], axis=0)
        term = term + mm_tn(att[count:], other)
    half = mine_ref.shape[0]
    term = term.astype(BF16)
    mine_ref[...] = term[:half]
    theirs_ref[...] = term[half:]


def middle_back_kernel(
    order_ref, up_ref, mod_ref, middle_ref, rows_ref, weight, grad_ref
):
    middle = middle_ref[...]
    _, time, *_ = columns(middle.shape[1])
    back = behind(rows_ref[:, : 3 * WIDTH], weight, time, time + 3 * WIDTH, order_ref)
    gain = 1.0 + mod_ref[1:2, :]
    grad = up_ref[...].astype(F32) + norm_back(middle, gain, back)
    grad_ref[...] = grad


def result_kernel(slots, index_ref, middle_ref, rows_ref, weight, result_ref):
    att = mm(rows_ref[:, 3 * WIDTH :], expander(index_ref[2:3, :])).astype(BF16)
    *_, out, stop = columns(middle_ref.shape[1])
    grown = ahead(att, weight, out, stop, slots)
    result_ref[...] = (middle_ref[...] + grown).astype(BF16)


def space_back_kernel(
    q_ref, kv_ref, probs_ref, att_grad_ref, dq_ref, own_ref, low_ref, high_ref
):
    span = low_ref.shape[0]
    keys, values = kv_ref[:, :WIDTH], kv_ref[:, WIDTH:]
    dquery, dkeys, dvalues = attention_back(
        spread(q_ref[...]), keys, values, probs_ref[...], att_grad_ref[...]
    )
    dq_ref[...] = dquery.astype(BF16)
    both = jnp.concatenate([dkeys, dvalues], axis=1)
    low_ref[...] = both[:span].astype(BF16)
    own_ref[...] = both[span : 3 * span]
    high_ref[...] = both[3 * span :].astype(BF16)


def start_back_kernel(
    order_ref, x_ref, mod_ref, grad_ref, dq_ref, own_ref, left, right, weight, out_ref
):
    x = x_ref[...].astype(F32)
    rim = jnp.concatenate([left[...], right[...]], axis=0).astype(F32)
    dkv = own_ref[...] + rim
    grads = jnp.concatenate([dq_ref[...].astype(F32), dkv], axis=1).astype(BF16)
    back = behind(grads, weight, 0, 3 * WIDTH, order_ref)
    gain = 1.0 + mod_ref[0:1, :]
    out_ref[...] = (grad_ref[...] + norm_back(x, gain, back)).astype(BF16)


VMEM = pl.BlockSpec(memory_space=pltpu.VMEM)
SMEM = pl.BlockSpec(memory_space=pltpu.SMEM)


HBM = pl.BlockSpec(memory_space=pltpu.HBM)


def call(kernel, name, scalars, arrays, weight, outs, scratch=(), far=(), grant=VMEM_LIMIT, cost=None):
    plain = len(scalars) + len(arrays) + len(far)
    weight, tree = jax.tree.flatten(list(weight))

    def body(*refs):
        fixed, pieces = refs[:plain], refs[plain : plain + len(weight)]
        pieces = (jax.tree.unflatten(tree, pieces),) if pieces else ()
        kernel(*fixed, *pieces, *refs[plain + len(weight) :])

    outs = [jax.ShapeDtypeStruct(shape, kind) for shape, kind in outs]
    near = [pltpu.VMEM(array.shape, array.dtype) for array in far]
    if far:
        near.append(pltpu.SemaphoreType.DMA((len(far),)))
    specs = [SMEM] * len(scalars) + [VMEM] * len(arrays) + [HBM] * len(far) + [VMEM] * len(weight)
    return pl.pallas_call(
        body,
        name=name,
        in_specs=specs,
        out_specs=[VMEM] * len(outs),
        out_shape=outs,
        scratch_shapes=near + list(scratch),
        compiler_params=pltpu.CompilerParams(vmem_limit_bytes=grant),
        cost_estimate=cost,
    )(*scalars, *arrays, *far, *weight)


def swapped(array, axis, bit):
    count = lax.axis_size(axis)
    return lax.ppermute(array, axis, [(i, i ^ bit) for i in range(count)])


def added(a, b):
    return (a.astype(F32) + b.astype(F32)).astype(BF16)


def relative_rows(shard, tile_at, clip_at, tiles, clips):
    block, inner = np.arange(clips * tiles * shard) // shard, np.arange(clips * tiles * shard) % shard
    low, apart, high = block // (2 * clips), block // 2 % clips, block % 2
    tile, clip = tile_at ^ (low + 2 * high), (clip_at + clips - apart) % clips
    return (clip * tiles + tile) * shard + inner


def local(
    latents,
    upstream,
    modulation,
    space_qkv,
    space_out,
    time_qkv,
    time_out,
    space_pattern,
    time_mask,
):
    seq, tiles, clips = lax.axis_size("seq"), lax.axis_size("tile"), lax.axis_size("dp")
    own, model = latents.shape[2], latents.shape[3]
    span, half = own // 2, own // 2
    shard = space_out.shape[0]
    x = latents.reshape(own, model)
    up = upstream.reshape(own, model)
    mod = modulation.reshape(modulation.shape[1:])
    tile_at, seq_at, clip_at = lax.axis_index("tile"), lax.axis_index("seq"), lax.axis_index("dp")
    side = seq_at if seq == 2 else jnp.zeros((), jnp.int32)
    place = jnp.stack([tile_at, side]).astype(jnp.int32)

    square = seq == 2 and tiles == 4
    hold = lax.optimization_barrier
    width = 6 * WIDTH + model
    own_w, half_w = call(
        pack_kernel, "pack", (), (), (),
        (((2 * shard, width), BF16), ((2 * shard, width // 2), BF16)),
        far=(space_qkv, time_qkv, space_out, time_out), grant=PACK_LIMIT,
    )
    if square:
        order = relative_rows(2 * shard, tile_at, clip_at, tiles, clips)
    else:
        order = jnp.arange(model)

    inner = order // (2 * shard) * shard + order % shard
    later = order % (2 * shard) >= shard
    space_rows = jnp.where((order >= 0) & ~later, inner, -1)
    time_rows = jnp.where((order >= 0) & later, inner, -1)
    index = jnp.stack([order, space_rows, time_rows]).astype(jnp.int32)
    near = np.arange(WIDTH) // shard
    bits = tiles.bit_length() - 1
    first = near // clips
    rel_tile = sum(((first >> b) & 1) << (bits - 1 - b) for b in range(bits))
    owner = (clip_at ^ (near % clips)) * tiles + (tile_at ^ rel_tile)
    terms = (owner * shard + np.arange(WIDTH) % shard).astype(jnp.int32).reshape(1, WIDTH)

    rise = [(i, i + 1) for i in range(tiles - 1)]
    fall = [(i + 1, i) for i in range(tiles - 1)]

    def rims(rows):
        before = lax.ppermute(rows[span:], "tile", rise)
        return before, lax.ppermute(rows[:span], "tile", fall)

    def joined(blocks):
        layout = [[(start, stop) for _, start, stop in block] for block in blocks]
        arrays = [array for block in blocks for array, _, _ in block]
        shape = (len(blocks) * 2 * shard, columns(model)[-1])
        return functools.partial(join_kernel, layout), arrays, (shape, BF16)

    def whole(array):
        return (array, 0, array.shape[1])

    (made,) = call(order_kernel, "order", (), (index,), (), (((model, model), BF16),))

    def normed_of(order, before, rows, after):
        return call(
            normed_kernel, "normed", (), (order, before, rows, after, mod), (),
            (((2 * own, model), BF16),),
        )[0]

    if square:
        lanes = width // 2
        cut = lanes // 256 * 128

        def onward(piece):
            return lax.ppermute(piece, "dp", [(i, (i + 1) % clips) for i in range(clips)])

        def near_rows(piece, sides):
            return [(piece, 0, lanes), (sides[1], 0, lanes)]

        def far_rows(sides, later):
            low, high = (part.shape[1] for part in later)
            return [
                (sides[0], 0, lanes),
                (later[0], low - cut, low), (later[1], high - (lanes - cut), high),
            ]

        def sends(piece, by_tile, by_seq, blocks=()):
            arrays = [by_tile, by_seq] if piece is None else [piece, by_tile, by_seq]
            at, count = (0 if piece is None else lanes), len(arrays)
            join, parts, shape = joined(blocks)

            def kernel(place_ref, *refs):
                sides, earlier = refs[:count], refs[count : count + len(parts)]
                outs = refs[count + len(parts) :]
                sides = sides if piece is not None else (None,) + sides
                send_kernel((cut, lanes), *sides, *outs[:2])
                if parts:
                    join(place_ref, *earlier, outs[2])

            outs = [((2 * shard, at + cut), BF16), ((2 * shard, at + lanes - cut), BF16)]
            if parts:
                outs.append(shape)
            over_tile, over_seq, *group = call(
                kernel, "send", (place,), (*arrays, *parts), (), outs
            )
            return group, (swapped(over_tile, "tile", 2), swapped(over_seq, "seq", 1))

        across = swapped(own_w, "tile", 2)
        piece, other_x, early = hold((onward(half_w), swapped(x, "seq", 1), x))
        pieces, came, groups, others = [piece], [], [], []
        for step in range(clips):
            piece = pieces[step] if step < clips - 1 else None
            following = onward(piece) if step < clips - 2 else ()
            if step == 0:
                moves = swapped(piece, "tile", 2), swapped(piece, "seq", 1)
                later_up, _ = hold((up, piece))
                moves, across, other_up = hold((moves, across, swapped(later_up[:half], "seq", 1)))
            else:
                blocks = [[whole(own_w)], [whole(across)]] if step == 2 else []
                if step > 1:
                    blocks.append(near_rows(pieces[step - 2], came[step - 2]))
                    blocks.append(far_rows(came[step - 2], came[step - 1]))
                if step == clips - 1:
                    blocks.append(near_rows(pieces[step - 1], came[step - 1]))
                group, moves = sends(piece, *came[-1], blocks)
                if group:
                    groups += group
                    others.append(swapped(groups[-1], "tile", 1))
            if step == 1:
                moves, made = hold((moves, made))
            if step == clips - 2:
                early, *_ = hold((early, came[-1]))
                moves, before, after = hold((moves, *rims(early)))
            if step == clips - 1:
                normed = normed_of(made, before, x, after)
                at = groups[0].shape[0]
                (partial,) = call(
                    functools.partial(early_kernel, [(0, at), (at, groups[1].shape[0]), (model // 2, at)]),
                    "space_early", (), (normed,), [*groups[:2], others[0]],
                    (((2 * own, 3 * WIDTH), F32),), cost=SHORT,
                )
                late = normed
                moves, normed, partial = hold((moves, normed, partial))
            moves, following, others = hold((moves, following, others))
            came.append(moves)
            if step < clips - 2:
                pieces.append(following)
        order = made
        late_up, _ = hold((up, late))
        other_up = other_up, swapped(late_up[half:], "seq", 1)
        join, parts, shape = joined([far_rows(came[-2], came[-1])])
        groups += call(join, "join", (place,), parts, (), (shape,))
        others.append(swapped(groups[-1], "tile", 1))
        weight = groups + others
        late, partial = [2, 4, 5], (partial,)
    else:
        before, after = rims(x)
        order = made
        normed = normed_of(order, before, x, after)
        join, parts, shape = joined([[whole(own_w)]])
        (laid,) = call(join, "join", (place,), parts, (), (shape,))
        weight = [lax.all_gather(laid, ("dp", "tile"), axis=0, tiled=True)]
        late, partial = [0], ()
    ends = np.cumsum([0] + [part.shape[0] for part in weight]).tolist()
    slots = [(at, part.shape[0]) for at, part in zip(ends, weight)]

    query, window, att, probs = call(
        functools.partial(forward_kernel, tiles, slots, late), "forward", (place, space_pattern),
        (normed,) + partial, weight,
        (
            ((own, WIDTH), BF16), ((2 * own, 2 * WIDTH), BF16), ((own, WIDTH), BF16),
            ((HEADS * own, 2 * own), F32),
        ),
        cost=SHORT,
    )
    middle, rows = call(
        functools.partial(middle_kernel, slots), "middle", (), (index, order, x, mod, att), weight,
        (((own, model), F32), ((own, 3 * WIDTH), BF16)), cost=SHORT,
    )
    if square:
        ups = (up,) + other_up
        other_att = swapped(att, "seq", 1)
    else:
        def turned(array):
            parts = array.reshape(seq, own // seq, array.shape[1])
            parts = lax.all_to_all(parts, "seq", split_axis=0, concat_axis=0, tiled=True)
            return parts.reshape(array.shape)

        ups = (turned(up),)
    (time_att_grad,) = call(
        functools.partial(att_grad_kernel, len(ups), 2), "att_grad", (), (index,) + ups, weight,
        ((((2 if square else 1) * own, WIDTH), BF16),),
    )
    if square:
        rows, att = call(
            functools.partial(time_pair_kernel, slots), "time_att", (place, time_mask),
            (index, order, mod, other_x, other_att, rows, time_att_grad), weight,
            (((own, 4 * WIDTH), BF16), ((2 * own, WIDTH), BF16)),
        )
    else:
        token = jnp.arange(own)
        frame, patch = token // (own // seq), token % (own // seq)
        seen = jnp.take(jnp.take(time_mask, frame, axis=0), frame, axis=1) == 1
        seen = (seen & (frame[None, :] < frame[:, None])) | (frame[None, :] == frame[:, None])
        allowed = (seen & (patch[None, :] == patch[:, None])).astype(jnp.int32)
        (rows,) = call(
            time_att_kernel, "time_att", (), (allowed, turned(rows), time_att_grad), (),
            (((own, 4 * WIDTH), BF16),),
        )
        att = rows[:, 3 * WIDTH :]
        rows = turned(rows)
    mine, theirs = call(
        functools.partial(term_kernel, len(ups)), "term", (), (terms, att) + ups, (),
        (((WIDTH // 2, model), BF16),) * 2,
    )

    (grad,) = call(
        middle_back_kernel, "middle_back", (), (order, up, mod, middle, rows), weight,
        (((own, model), F32),),
    )
    (att_grad,) = call(
        functools.partial(att_grad_kernel, 1, 1), "space_grad", (), (index, grad), weight,
        (((own, WIDTH), BF16),),
    )
    dq, own_grads, to_left, to_right = call(
        space_back_kernel, "space_back", (), (query, window, probs, att_grad), (),
        (
            ((own, WIDTH), BF16), ((own, 2 * WIDTH), F32),
            ((span, 2 * WIDTH), BF16), ((span, 2 * WIDTH), BF16),
        ),
    )
    from_left = lax.ppermute(to_right, "tile", rise)
    from_right = lax.ppermute(to_left, "tile", fall)
    (start_grad,) = call(
        start_back_kernel, "start_back", (),
        (order, x, mod, grad, dq, own_grads, from_left, from_right), weight,
        (((own, model), BF16),),
    )
    late, _ = hold((rows, start_grad))
    (result,) = call(
        functools.partial(result_kernel, slots), "result", (),
        (index, middle, late), weight, (((own, model), BF16),),
    )

    def ended(came, kernel):
        return hold((came, kernel))[0]

    ends, bit = [grad], 1
    while bit < tiles:
        came = ended(swapped(theirs, "tile", bit), ends.pop(0) if ends else dq)
        mine = added(mine, came)
        bit *= 2
        if bit < tiles:
            rows = mine.shape[0] // 2
            mine, theirs = mine[:rows], mine[rows:]
    came = [swapped(mine[by * shard : (by + 1) * shard], "dp", by) for by in range(1, clips)]
    came = [ended(came[0], result)] + ended(came[1:], start_grad)
    total = mine[:shard].astype(F32)
    for part in came:
        total = total + part.astype(F32)
    if not square:
        total = lax.psum(total.astype(BF16), "seq").astype(F32)
    return (result.reshape(latents.shape), start_grad.reshape(latents.shape), total)


def solution(mesh):
    in_specs = (
        P("dp", "seq", "tile", None),
        P("dp", "seq", "tile", None),
        P("dp", None, None),
        P(("dp", "tile"), None),
        P(("dp", "tile"), None),
        P(("dp", "tile"), None),
        P(("dp", "tile"), None),
        P("tile", None),
        P(),
    )
    out_specs = (
        P("dp", "seq", "tile", None),
        P("dp", "seq", "tile", None),
        P(("dp", "tile"), None),
    )
    return jax.shard_map(local, mesh=mesh, in_specs=in_specs, out_specs=out_specs, check_vma=False)
```
